32 devices in a mesh: expert: 8 (over z, core), mp: 4 (over y, x).
Axes of the slice: x: 2, y: 2, z: 4, core: 2. Of those that a mesh axis runs over, the one named last changes fastest.
Arguments:
- tokens: bfloat16 [1024, 4096], P('expert', 'mp'), may hold values from -6 to 6
- expert_ids: int32 [1024, 1], P('expert'), may hold values from 0 to 7; in each aligned block of 128 rows (0 to 127, 128 to 255, ...) at most 32 rows name the same one
- seq_lengths: int32 [8], P('expert'), may hold values from 64 to 128, as said below
- hidden_cotangent: bfloat16 [8, 256, 6144], P('expert', None, 'mp'), may hold values from -6 to 6
- w_in: bfloat16 [8, 4096, 6144], P('expert', None, 'mp'), may hold values from -0.09375 to 0.09375
Outputs:
- grad_tokens: bfloat16 [1024, 4096], P('expert', 'mp')
The draws below stay inside these ranges and needn't reach their ends.
Inputs may be any that keep to these rules, and one draw needn't show every extreme that they name: `expert_ids`: in each aligned block of 128 rows no expert is named by more than 32 rows, a bound that some block reaches. `seq_lengths`: some sequence is full and some has exactly 64 live positions.
All inputs are finite; a program needn't handle non-finite values.
Results may differ from the reference program's by a relative error of at most 0.014.
Values may be sent and summed in bfloat16 or wider, within the bound.
A program may use at most 64 MiB of HBM per device.

```python
import math
import jax
import jax.numpy as jnp
import numpy as np
from jax import lax

D = 4096
FF = 6144
SEQ_LEN = 128
TOK_DEV = 128
EXPERTS = 8
CAP = 32
SLOTS = 256
TOKENS = 1024
SEQS = 8
N_EXPERT = 8
N_MP = 4


def draw_seq_lengths(key, part):
    key_one, key_two, key_three = jax.random.split(jax.random.fold_in(key, 17), 3)
    lengths = jax.random.randint(key_one, (SEQS,), SEQ_LEN // 2, SEQ_LEN + 1)
    first = jax.random.randint(key_two, (), 0, SEQS)
    second = (first + 1 + jax.random.randint(key_three, (), 0, SEQS - 1)) % SEQS
    lengths = lengths.at[first].set(SEQ_LEN).at[second].set(SEQ_LEN // 2)
    return lengths.astype(jnp.int32)


def block_scale(rng, shape, shards, smallest, largest):
    def one(dim, blocks):
        steps = jax.random.uniform(jax.random.fold_in(jax.random.fold_in(rng, 6), dim), (blocks,), jnp.float32, smallest / len(shards), largest / len(shards))
        return jnp.repeat(jnp.exp(steps), shape[dim] // blocks).reshape((-1,) + (1,) * (len(shape) - dim - 1))

    loudness = one(*shards[0])
    for cut in shards[1:]:
        loudness = loudness * one(*cut)
    return loudness


def shared_out(rng, own, number, rows, count, top, bound, skew):
    order = jax.random.permutation(rng, count)
    crowded, usual = load_shares(count, rows * top, bound, skew, True), load_shares(count, rows * top, bound, skew, False)
    places = jnp.arange(count)

    def named(tallies, offset_by):
        used = int((tallies > 0).sum())
        fixed = max(1, used // 4)
        moved = fixed + (places - fixed + offset_by * (used - fixed)) % max(1, count - fixed)
        return jnp.zeros((count,), jnp.int32).at[order[jnp.where(places < fixed, places, moved)]].set(jnp.asarray(tallies, jnp.int32))

    tallies = jnp.where(number % 4 == 0, named(crowded, number // 4), named(usual, number - number // 4 - 1))
    mixed = jax.random.permutation(jax.random.fold_in(own, 3), count)
    giver, sink = mixed[0:count // 2 * 2:2], mixed[1:count // 2 * 2:2]
    room = jnp.minimum(tallies[giver] - 1, bound - tallies[sink]) // 2
    room = jnp.where((giver == order[0]) | (sink == order[0]) | (tallies[sink] == 0), 0, jnp.maximum(room, 0))
    moved = jax.random.randint(jax.random.fold_in(own, 4), (count // 2,), 0, 1 << 20) % (room + 1)
    tallies = tallies.at[giver].add(-moved).at[sink].add(moved)
    labels = jnp.searchsorted(jnp.cumsum(tallies), jnp.arange(rows * top), side="right").astype(jnp.int32)
    grid = labels.reshape(top, rows).T
    grid = grid[jax.random.permutation(jax.random.fold_in(own, 1), rows)]
    offset_by = jax.random.randint(jax.random.fold_in(own, 2), (rows, 1), 0, top)
    return jnp.take_along_axis(grid, (jnp.arange(top)[None, :] + offset_by) % top, axis=1)


def load_shares(amount, total, most, slope, full):
    loads = [(1 << 20) // math.isqrt(rank ** slope) + 1 for rank in range(1, amount + 1)]
    largest = most if full else min(most, max(-(-total // amount), total * loads[0] // sum(loads)))
    least = 1 if total - largest >= amount - 1 else 0
    counts, spare = [largest] + [least] * (amount - 1), total - largest - least * (amount - 1)
    while spare > 0:
        candidates = [i for i in range(1, amount) if counts[i] < largest] or [i for i in range(1, amount) if counts[i] < most]
        pool, budget = sum([loads[i] for i in candidates]), spare
        for i in candidates:
            extra = min(most - counts[i], max(1, budget * loads[i] // pool), spare)
            counts[i] = counts[i] + extra
            spare = spare - extra
    return np.array(counts)


def scatter_about(rng, extent, spread, bound, cuts=(), kind=jnp.bfloat16):
    array = jax.random.normal(rng, extent, jnp.float32) * spread
    if len(cuts) > 0:
        array = block_scale(rng, extent, cuts, -0.22, 0.18) * array
    return jnp.clip(array, min=-bound, max=bound).astype(kind)


def setup_inputs(seed: int = 0) -> dict:
    key_list = jax.random.split(jax.random.key(seed), 6)
    tokens = scatter_about(key_list[0], (TOKENS, D), 1.0, 6.0, ((0, 8), (1, 4)))
    expert_ids_keys = jax.random.split(jax.random.fold_in(key_list[1], 1), TOKENS // TOK_DEV)
    expert_ids_turns = jax.random.permutation(jax.random.fold_in(key_list[1], 3), TOKENS // TOK_DEV)
    expert_ids = jax.vmap(lambda own, number: shared_out(jax.random.fold_in(key_list[1], 2), own, number, TOK_DEV, EXPERTS, 1, CAP, 2))(expert_ids_keys, expert_ids_turns).reshape((TOKENS, 1))
    seq_lengths = draw_seq_lengths(jax.random.fold_in(key_list[5], 71), 0)
    hidden_cotangent = scatter_about(key_list[3], (EXPERTS, SLOTS, FF), 1.0, 6.0, ((0, 8), (2, 4)))
    w_in = scatter_about(key_list[4], (EXPERTS, D, FF), D ** -0.5, 0.09375, ((0, 8), (2, 4)))
    return {"tokens": tokens, "expert_ids": expert_ids, "seq_lengths": seq_lengths, "hidden_cotangent": hidden_cotangent, "w_in": w_in}


def gelu_slope(preact):
    coeff = math.sqrt(2.0 / math.pi)
    squashed = jnp.tanh(coeff * (preact + 0.044715 * preact * preact * preact))
    return 0.5 * (1.0 + squashed) + 0.5 * preact * (1.0 - squashed * squashed) * coeff * (1.0 + 3.0 * 0.044715 * preact * preact)

def reference(tokens, expert_ids, seq_lengths, hidden_cotangent, w_in):
    slot_count = N_EXPERT * CAP
    position = jnp.arange(TOKENS, dtype=jnp.int32)
    seq_length = seq_lengths[position // SEQ_LEN]
    live_mask = (position % SEQ_LEN < seq_length).reshape(N_EXPERT, TOK_DEV)
    expert_row = expert_ids[:, 0].reshape(N_EXPERT, TOK_DEV)
    onehot = ((expert_row[:, :, None] == jnp.arange(EXPERTS, dtype=jnp.int32)[None, None, :]) & live_mask[:, :, None]).astype(jnp.int32)
    slot_rank = lax.optimization_barrier(jnp.sum(jnp.cumsum(onehot, axis=1) * onehot, axis=2)) - 1
    source = jnp.arange(N_EXPERT, dtype=jnp.int32)[:, None]
    target = jnp.where(live_mask, expert_row * slot_count + source * CAP + slot_rank, EXPERTS * slot_count).reshape(-1).astype(jnp.int32)
    buffer = jnp.zeros((EXPERTS * slot_count + 1, D), tokens.dtype).at[target].set(tokens)
    slot_tokens = buffer[:-1].reshape(EXPERTS, slot_count, D)

    def per_expert(inputs):
        features, cotangent, weight = inputs
        pre_act = jnp.dot(features, weight, preferred_element_type=jnp.float32)
        hidden_grad = (cotangent.astype(jnp.float32) * gelu_slope(pre_act)).astype(jnp.bfloat16)
        blocks = hidden_grad.reshape(slot_count, N_MP, FF // N_MP).astype(jnp.float32)
        weight_blocks = weight.reshape(D, N_MP, FF // N_MP).astype(jnp.float32)
        block_parts = jnp.einsum('rmf,dmf->mrd', blocks, weight_blocks).astype(jnp.bfloat16)
        block_parts = lax.optimization_barrier(block_parts)
        return lax.optimization_barrier(jnp.sum(block_parts.astype(jnp.float32), axis=0)).astype(jnp.bfloat16)
    slot_grads = lax.map(per_expert, (slot_tokens, hidden_cotangent, w_in))
    flat_grads = jnp.concatenate([slot_grads.reshape(EXPERTS * slot_count, D), jnp.zeros((1, D), jnp.bfloat16)], axis=0)
    return flat_grads[target]
```

```python
import functools
import math

import jax
import jax.numpy as jnp
from jax import lax
from jax.experimental import pallas as pl
from jax.experimental.pallas import tpu as pltpu
from jax.sharding import PartitionSpec as P

SEQ_LEN = 128
MESH = pl.DeviceIdType.MESH
ORDER = (0, 1, 4, 5, 6, 7, 2, 3)
TILE = 256
def gelu_slope(preact):
    coeff = math.sqrt(2.0 / math.pi)
    squashed = jnp.tanh(coeff * (preact + 0.044715 * preact * preact * preact))
    return 0.5 * (1.0 + squashed) + 0.5 * preact * (1.0 - squashed * squashed) * coeff * (
        1.0 + 3.0 * 0.044715 * preact * preact
    )


def per_device(tokens, expert_ids, seq_lengths, hidden_cotangent, w_in):
    tok_dev = tokens.shape[0]
    experts = w_in.shape[0] * lax.axis_size("expert")
    capacity = max(2, 2 * tok_dev // experts)
    position = jnp.arange(tok_dev, dtype=jnp.int32)
    seq_index = position // SEQ_LEN
    seq_length = jnp.sum(
        jnp.where(
            seq_index[:, None] == jnp.arange(seq_lengths.shape[0], dtype=jnp.int32)[None, :],
            seq_lengths[None, :],
            0,
        ),
        axis=1,
    )
    live_mask = position % SEQ_LEN < seq_length
    expert_row = expert_ids[:, 0]
    onehot = (
        (expert_row[:, None] == jnp.arange(experts, dtype=jnp.int32)[None, :]) & live_mask[:, None]
    ).astype(jnp.int32)
    slot_rank = jnp.sum(jnp.cumsum(onehot, axis=0) * onehot, axis=1) - 1
    target = jnp.where(live_mask, expert_row * capacity + slot_rank, experts * capacity)
    buffer = (
        jnp.zeros((experts * capacity + 1,) + tokens.shape[1:], tokens.dtype).at[target].set(tokens)
    )
    arrived = lax.all_to_all(
        buffer[:-1].reshape((experts, capacity) + tokens.shape[1:]),
        "expert",
        split_axis=0,
        concat_axis=0,
        tiled=True,
    )
    slot_count = arrived.shape[0] * capacity
    features = lax.all_gather(
        arrived.reshape(slot_count, arrived.shape[2]), "mp", axis=1, tiled=True
    )
    weight = w_in[0]
    pre_act = jnp.dot(features, weight, preferred_element_type=jnp.float32)
    hidden_grad = (hidden_cotangent[0].astype(jnp.float32) * gelu_slope(pre_act)).astype(
        jnp.bfloat16
    )
    partial_value = lax.dot_general(
        hidden_grad, weight, (((1,), (1,)), ((), ())), preferred_element_type=jnp.float32
    ).astype(jnp.bfloat16)
    partial_value = lax.optimization_barrier(partial_value)
    summed = lax.psum_scatter(
        partial_value.astype(jnp.float32).astype(jnp.bfloat16),
        "mp",
        scatter_dimension=1,
        tiled=True,
    )
    returned = lax.all_to_all(
        summed.reshape(arrived.shape[0], capacity, summed.shape[1]),
        "expert",
        split_axis=0,
        concat_axis=0,
        tiled=True,
    )
    flat_rows = returned.reshape((experts * capacity,) + returned.shape[2:])
    padded = jnp.concatenate(
        [flat_rows, jnp.zeros((1,) + flat_rows.shape[1:], flat_rows.dtype)], axis=0
    )
    return padded[target]


def flip(index, difference, bits):
    total = 0
    for bit in range(bits):
        value = lax.rem(index // (1 << bit), 2)
        total = total + (1 << bit) * ((1 - value) if difference >> bit & 1 else value)
    return total


def kernel(
    cap,
    tokens_ref,
    ids_ref,
    lengths_ref,
    cot_hbm,
    w_hbm,
    out_ref,
    w_v,
    cot_v,
    send_rows,
    feats,
    parts,
    hidden,
    combine,
    diag_in,
    direct_in,
    sum_in,
    sum_out,
    done_rows,
    back_rows,
    local_sem,
    send_sem,
    recv_sem,
):
    expert, place = lax.axis_index("expert"), lax.axis_index("mp")
    peers = [flip(expert, k, 3) for k in ORDER]
    side = [None, (expert, flip(place, 1, 2)), (expert, flip(place, 2, 2))]
    tok, width = tokens_ref.shape
    ff = w_v.shape[2]
    half = cap // 2
    first, second = pl.ds(0, half), pl.ds(half, half)

    barrier = pltpu.get_barrier_semaphore()
    greeted = [(peer, place) for peer in peers[1:]] + side[1:]
    for device in greeted:
        pl.semaphore_signal(barrier, inc=1, device_id=device, device_id_type=MESH)

    loads = []
    for j in range(4):
        start = pl.multiple_of(flip(place, j, 2) * width, width)
        loads.append(
            pltpu.make_async_copy(w_hbm.at[0, pl.ds(start, width)], w_v.at[j], local_sem.at[j])
        )
    cot_loads = []
    for p in range(8):
        start = pl.multiple_of(peers[p] * cap, cap)
        cot_loads.append(
            pltpu.make_async_copy(
                cot_hbm.at[0, pl.ds(start, cap)], cot_v.at[p], local_sem.at[4 + p]
            )
        )
    for load in loads + cot_loads:
        load.start()

    position = lax.broadcasted_iota(jnp.int32, (tok, 1), 0)
    limit = jnp.zeros((tok, 1), jnp.int32)
    for i in range(lengths_ref.shape[0]):
        limit = jnp.where(position // SEQ_LEN == i, lengths_ref[i], limit)
    live = position % SEQ_LEN < limit
    away = jnp.bitwise_xor(ids_ref[...], expert)
    rank_of = jnp.zeros((tok, 1), jnp.int32)
    for p, k in enumerate(ORDER):
        rank_of = jnp.where(away == k, p, rank_of)
    lanes = lax.broadcasted_iota(jnp.int32, (tok, 128), 1)
    onehot = jnp.where((lanes == rank_of) & live, 1.0, 0.0)
    before = lax.broadcasted_iota(jnp.int32, (tok, tok), 1) <= lax.broadcasted_iota(
        jnp.int32, (tok, tok), 0
    )
    counts = jnp.dot(
        jnp.where(before, 1.0, 0.0).astype(jnp.bfloat16),
        onehot.astype(jnp.bfloat16),
        preferred_element_type=jnp.float32,
    )
    slot = jnp.sum(counts * onehot, axis=1, keepdims=True) - 1.0 + (rank_of * cap).astype(
        jnp.float32
    )
    slots = lax.broadcasted_iota(jnp.int32, (tok, 8 * cap), 1).astype(jnp.float32)
    chosen = jnp.where((slots == slot) & live, 1.0, 0.0)
    combine[...] = chosen.astype(jnp.bfloat16)
    placed = jnp.dot(
        chosen.T.astype(jnp.bfloat16), tokens_ref[...], preferred_element_type=jnp.float32
    ).astype(jnp.bfloat16)
    feats[0, 0] = placed[:cap]
    for p in range(1, 8):
        send_rows[p] = placed[p * cap : (p + 1) * cap]

    pl.semaphore_wait(barrier, len(greeted))

    started = []
    numbers = iter(range(1000))

    def remote(source, target, device):
        n = next(numbers)
        return pltpu.make_async_remote_copy(
            src_ref=source,
            dst_ref=target,
            send_sem=send_sem.at[n],
            recv_sem=recv_sem.at[n],
            device_id=device,
            device_id_type=MESH,
        )

    def go(copy):
        copy.start()
        started.append(copy)

    out_copies = [None] + [
        remote(send_rows.at[p], feats.at[0, p], (peers[p], place)) for p in range(1, 8)
    ]
    back_copies = [None] + [
        remote(done_rows.at[p], back_rows.at[p], (peers[p], place)) for p in range(1, 8)
    ]
    pairs = [pl.ds(2 * q, 2) for q in range(4)]
    gather = [
        [None] + [remote(feats.at[0, pair], feats.at[d, pair], side[d]) for d in (1, 2)]
        for pair in pairs
    ]
    relay = [
        [
            None,
            remote(feats.at[2, pair, second], feats.at[3, pair, second], side[1]),
            remote(feats.at[1, pair, first], feats.at[3, pair, first], side[2]),
        ]
        for pair in pairs
    ]
    rows = [None, first, second]
    diag = [
        [None]
        + [remote(parts.at[3, pair, rows[d]], diag_in.at[d - 1, pair], side[d]) for d in (1, 2)]
        for pair in pairs
    ]
    direct = [
        [None]
        + [remote(parts.at[d, pair, rows[d]], direct_in.at[d - 1, pair], side[d]) for d in (1, 2)]
        for pair in pairs
    ]
    summed = [
        [None]
        + [remote(sum_out.at[d - 1, pair], sum_in.at[d - 1, pair], side[d]) for d in (1, 2)]
        for pair in pairs
    ]

    for p in range(1, 8):
        go(out_copies[p])

    def gather_start(q):
        for p in (2 * q, 2 * q + 1):
            if p:
                out_copies[p].wait_recv()
        go(gather[q][1])
        go(gather[q][2])

    def gather_relay(q):
        gather[q][1].wait_recv()
        go(relay[q][2])
        gather[q][2].wait_recv()
        go(relay[q][1])

    def gather_end(q):
        relay[q][1].wait_recv()
        relay[q][2].wait_recv()

    def hidden_tiles(g, low, high):
        group = pl.ds(4 * g, 4)

        @pl.loop(low, high)
        def _(n):
            columns = pl.ds(pl.multiple_of(n * TILE, TILE), TILE)
            total = jnp.zeros((4 * cap, TILE), jnp.float32)
            for j in range(4):
                total += jnp.dot(
                    feats[j, group].reshape(4 * cap, width),
                    w_v[j, :, columns],
                    preferred_element_type=jnp.float32,
                )
            cotangent = cot_v[group, :, columns].reshape(4 * cap, TILE).astype(jnp.float32)
            hidden[:, columns] = (cotangent * gelu_slope(total)).astype(jnp.bfloat16)

    def part_tiles(g, j):
        group = pl.ds(4 * g, 4)

        @pl.loop(0, width // TILE)
        def _(n):
            columns = pl.ds(pl.multiple_of(n * TILE, TILE), TILE)
            block = lax.dot_general(
                hidden[...],
                w_v[j, columns, :],
                (((1,), (1,)), ((), ())),
                preferred_element_type=jnp.float32,
            )
            parts[j, group, :, columns] = block.astype(jnp.bfloat16).reshape(4, cap, TILE)

    def sum_step(q):
        pair = pairs[q]
        for d in (1, 2):
            diag[q][d].wait_recv()
            other = 3 - d
            sum_out[other - 1, pair] = (
                parts[other, pair, rows[d]].astype(jnp.float32)
                + diag_in[d - 1, pair].astype(jnp.float32)
            ).astype(jnp.bfloat16)
            go(summed[q][other])

    def final_step(q):
        pair = pairs[q]
        for d in (1, 2):
            direct[q][d].wait_recv()
            summed[q][3 - d].wait_recv()
            total = (
                parts[0, pair, rows[d]].astype(jnp.float32)
                + direct_in[d - 1, pair].astype(jnp.float32)
                + sum_in[2 - d, pair].astype(jnp.float32)
            ).astype(jnp.bfloat16)
            done_rows[pair, rows[d]] = total
        for p in (2 * q, 2 * q + 1):
            if p:
                go(back_copies[p])
            else:
                back_rows[0] = done_rows[0]

    tiles = ff // TILE
    gather_start(0)
    gather_start(1)
    gather_relay(0)
    gather_start(2)
    gather_relay(1)
    gather_start(3)
    for load in loads + cot_loads:
        load.wait()
    gather_end(0)
    gather_end(1)
    hidden_tiles(0, 0, tiles // 2)
    gather_relay(2)
    hidden_tiles(0, tiles // 2, tiles)
    part_tiles(0, 3)
    for q in (0, 1):
        go(diag[q][1])
        go(diag[q][2])
    gather_relay(3)
    part_tiles(0, 1)
    for q in (0, 1):
        go(direct[q][1])
    part_tiles(0, 2)
    for q in (0, 1):
        go(direct[q][2])
    sum_step(0)
    part_tiles(0, 0)
    sum_step(1)
    gather_end(2)
    gather_end(3)
    hidden_tiles(1, 0, tiles // 2)
    final_step(0)
    hidden_tiles(1, tiles // 2, tiles)
    part_tiles(1, 3)
    for q in (2, 3):
        go(diag[q][1])
        go(diag[q][2])
    final_step(1)
    part_tiles(1, 1)
    for q in (2, 3):
        go(direct[q][1])
    part_tiles(1, 2)
    for q in (2, 3):
        go(direct[q][2])
    sum_step(2)
    sum_step(3)
    part_tiles(1, 0)
    final_step(2)
    final_step(3)
    for p in range(1, 8):
        back_copies[p].wait_recv()
    out_ref[...] = jnp.dot(
        combine[...],
        back_rows[...].reshape(8 * cap, width),
        preferred_element_type=jnp.float32,
    ).astype(out_ref.dtype)
    for copy in started:
        copy.wait_send()


def one_kernel(tokens, expert_ids, seq_lengths, hidden_cotangent, w_in):
    tok, width = tokens.shape
    ff = w_in.shape[2]
    cap = hidden_cotangent.shape[1] // 8
    half = cap // 2
    bf16 = jnp.bfloat16
    copies = 7 + 7 + 4 * 10
    vmem, anywhere = pl.BlockSpec(memory_space=pltpu.VMEM), pl.BlockSpec(memory_space=pl.ANY)
    return pl.pallas_call(
        functools.partial(kernel, cap),
        out_shape=jax.ShapeDtypeStruct((tok, width), tokens.dtype),
        in_specs=[vmem, vmem, pl.BlockSpec(memory_space=pltpu.SMEM), anywhere, anywhere],
        out_specs=vmem,
        scratch_shapes=[
            pltpu.VMEM((4, width, ff), bf16),
            pltpu.VMEM((8, cap, ff), bf16),
            pltpu.VMEM((8, cap, width), bf16),
            pltpu.VMEM((4, 8, cap, width), bf16),
            pltpu.VMEM((4, 8, cap, width), bf16),
            pltpu.VMEM((4 * cap, ff), bf16),
            pltpu.VMEM((tok, 8 * cap), bf16),
            pltpu.VMEM((2, 8, half, width), bf16),
            pltpu.VMEM((2, 8, half, width), bf16),
            pltpu.VMEM((2, 8, half, width), bf16),
            pltpu.VMEM((2, 8, half, width), bf16),
            pltpu.VMEM((8, cap, width), bf16),
            pltpu.VMEM((8, cap, width), bf16),
            pltpu.SemaphoreType.DMA((12,)),
            pltpu.SemaphoreType.DMA((copies,)),
            pltpu.SemaphoreType.DMA((copies,)),
        ],
        compiler_params=pltpu.CompilerParams(
            collective_id=0, has_side_effects=True, vmem_limit_bytes=48 << 20
        ),
        cost_estimate=pl.CostEstimate(
            flops=4 * 8 * cap * 4 * width * ff,
            bytes_accessed=2 * 4 * width * ff,
            transcendentals=8 * cap * ff,
        ),
    )(tokens, expert_ids, seq_lengths, hidden_cotangent, w_in)


def solution(mesh):
    in_specs = (
        P("expert", "mp"),
        P("expert", None),
        P("expert"),
        P("expert", None, "mp"),
        P("expert", None, "mp"),
    )
    out_specs = P("expert", "mp")
    small = mesh.shape["mp"] == 4 and mesh.shape["expert"] == 8
    return jax.shard_map(
        one_kernel if small else per_device,
        mesh=mesh,
        in_specs=in_specs,
        out_specs=out_specs,
        check_vma=False,
    )
```

```python
import functools
import math

import jax
import jax.numpy as jnp
from jax import lax
from jax.experimental import pallas as pl
from jax.experimental.pallas import tpu as pltpu
from jax.sharding import PartitionSpec as P

SEQ_LEN = 128
MESH = pl.DeviceIdType.MESH
ORDER = (0, 1, 4, 5, 2, 3, 6, 7)
RETURN = (3, 1, 2, 0)
TILE = 512
def gelu_slope(preact):
    coeff = math.sqrt(2.0 / math.pi)
    squashed = jnp.tanh(coeff * (preact + 0.044715 * preact * preact * preact))
    return 0.5 * (1.0 + squashed) + 0.5 * preact * (1.0 - squashed * squashed) * coeff * (
        1.0 + 3.0 * 0.044715 * preact * preact
    )


def per_device(tokens, expert_ids, seq_lengths, hidden_cotangent, w_in):
    tok_dev = tokens.shape[0]
    experts = w_in.shape[0] * lax.axis_size("expert")
    capacity = max(2, 2 * tok_dev // experts)
    position = jnp.arange(tok_dev, dtype=jnp.int32)
    seq_index = position // SEQ_LEN
    seq_length = jnp.sum(
        jnp.where(
            seq_index[:, None] == jnp.arange(seq_lengths.shape[0], dtype=jnp.int32)[None, :],
            seq_lengths[None, :],
            0,
        ),
        axis=1,
    )
    live_mask = position % SEQ_LEN < seq_length
    expert_row = expert_ids[:, 0]
    onehot = (
        (expert_row[:, None] == jnp.arange(experts, dtype=jnp.int32)[None, :]) & live_mask[:, None]
    ).astype(jnp.int32)
    slot_rank = jnp.sum(jnp.cumsum(onehot, axis=0) * onehot, axis=1) - 1
    target = jnp.where(live_mask, expert_row * capacity + slot_rank, experts * capacity)
    buffer = (
        jnp.zeros((experts * capacity + 1,) + tokens.shape[1:], tokens.dtype).at[target].set(tokens)
    )
    arrived = lax.all_to_all(
        buffer[:-1].reshape((experts, capacity) + tokens.shape[1:]),
        "expert",
        split_axis=0,
        concat_axis=0,
        tiled=True,
    )
    slot_count = arrived.shape[0] * capacity
    features = lax.all_gather(
        arrived.reshape(slot_count, arrived.shape[2]), "mp", axis=1, tiled=True
    )
    weight = w_in[0]
    pre_act = jnp.dot(features, weight, preferred_element_type=jnp.float32)
    hidden_grad = (hidden_cotangent[0].astype(jnp.float32) * gelu_slope(pre_act)).astype(
        jnp.bfloat16
    )
    partial_value = lax.dot_general(
        hidden_grad, weight, (((1,), (1,)), ((), ())), preferred_element_type=jnp.float32
    ).astype(jnp.bfloat16)
    partial_value = lax.optimization_barrier(partial_value)
    summed = lax.psum_scatter(
        partial_value.astype(jnp.float32).astype(jnp.bfloat16),
        "mp",
        scatter_dimension=1,
        tiled=True,
    )
    returned = lax.all_to_all(
        summed.reshape(arrived.shape[0], capacity, summed.shape[1]),
        "expert",
        split_axis=0,
        concat_axis=0,
        tiled=True,
    )
    flat_rows = returned.reshape((experts * capacity,) + returned.shape[2:])
    padded = jnp.concatenate(
        [flat_rows, jnp.zeros((1,) + flat_rows.shape[1:], flat_rows.dtype)], axis=0
    )
    return padded[target]


def flip(index, difference, bits):
    total = 0
    for bit in range(bits):
        value = lax.rem(index // (1 << bit), 2)
        total = total + (1 << bit) * ((1 - value) if difference >> bit & 1 else value)
    return total


def kernel(
    cap,
    tokens_hbm,
    ids_hbm,
    lengths_ref,
    cot_hbm,
    w_hbm,
    out_ref,
    tokens_ref,
    ids_ref,
    w_v,
    cot_v,
    send_rows,
    feats,
    parts,
    before_act,
    hidden,
    combine,
    diag_in,
    direct_in,
    sum_in,
    sum_out,
    done_rows,
    back_rows,
    local_sem,
    send_sem,
    recv_sem,
):
    expert, place = lax.axis_index("expert"), lax.axis_index("mp")
    peers = [flip(expert, k, 3) for k in ORDER]
    side = [None, (expert, flip(place, 1, 2)), (expert, flip(place, 2, 2))]
    tok, width = tokens_ref.shape
    ff = w_v.shape[2]
    half = cap // 2
    first, second = pl.ds(0, half), pl.ds(half, half)

    barrier = pltpu.get_barrier_semaphore()
    greeted = [(peer, place) for peer in peers[1:]] + side[1:]
    for device in greeted:
        pl.semaphore_signal(barrier, inc=1, device_id=device, device_id_type=MESH)

    inputs = [
        pltpu.make_async_copy(source, target, local_sem.at[12 + n])
        for n, (source, target) in enumerate(
            ((ids_hbm, ids_ref), (tokens_hbm, tokens_ref))
        )
    ]
    for load in inputs:
        load.start()
    loads = []
    for j in range(4):
        start = pl.multiple_of(flip(place, j, 2) * width, width)
        loads.append(
            pltpu.make_async_copy(w_hbm.at[0, pl.ds(start, width)], w_v.at[j], local_sem.at[j])
        )
    cot_loads = []
    for p in range(8):
        start = pl.multiple_of(peers[p] * cap, cap)
        cot_loads.append(
            pltpu.make_async_copy(
                cot_hbm.at[0, pl.ds(start, cap)], cot_v.at[p], local_sem.at[4 + p]
            )
        )

    position = lax.broadcasted_iota(jnp.int32, (1, tok), 1)
    limit = jnp.zeros((1, tok), jnp.int32)
    inputs[0].wait()
    for i in range(lengths_ref.shape[0]):
        limit = jnp.where(position // SEQ_LEN == i, lengths_ref[i], limit)
    live = position % SEQ_LEN < limit
    away = jnp.bitwise_xor(ids_ref[...], expert)
    rank_of = jnp.zeros((1, tok), jnp.int32)
    for p, k in enumerate(ORDER):
        rank_of = jnp.where(away == k, p, rank_of)
    rank_of = jnp.where(live, rank_of, -1)
    onehot = jnp.where(
        lax.broadcasted_iota(jnp.int32, (16, tok), 0) == rank_of, 1.0, 0.0
    )
    before = lax.broadcasted_iota(jnp.int32, (tok, tok), 0) <= lax.broadcasted_iota(
        jnp.int32, (tok, tok), 1
    )
    counts = jnp.dot(
        onehot.astype(jnp.bfloat16),
        jnp.where(before, 1.0, 0.0).astype(jnp.bfloat16),
        preferred_element_type=jnp.float32,
    )
    slot = jnp.sum(counts * onehot, axis=0, keepdims=True) - 1.0
    slot = jnp.where(live, slot + (rank_of * cap).astype(jnp.float32), -1.0)
    slots = lax.broadcasted_iota(jnp.int32, (8 * cap, tok), 0).astype(jnp.float32)
    chosen = jnp.where(slots == slot, 1.0, 0.0)
    inputs[1].wait()
    placed = jnp.dot(
        chosen.astype(jnp.bfloat16), tokens_ref[...], preferred_element_type=jnp.float32
    ).astype(jnp.bfloat16)
    feats[0, 0] = placed[:cap]
    for p in range(1, 8):
        send_rows[p] = placed[p * cap : (p + 1) * cap]

    pl.semaphore_wait(barrier, len(greeted))

    started = []
    numbers = iter(range(1000))

    def remote(source, target, device):
        n = next(numbers)
        return pltpu.make_async_remote_copy(
            src_ref=source,
            dst_ref=target,
            send_sem=send_sem.at[n],
            recv_sem=recv_sem.at[n],
            device_id=device,
            device_id_type=MESH,
        )

    def go(copy):
        copy.start()
        started.append(copy)

    out_copies = [None] + [
        remote(send_rows.at[p], feats.at[0, p], (peers[p], place)) for p in range(1, 8)
    ]
    back_copies = [None] + [
        remote(done_rows.at[p], back_rows.at[p], (peers[p], place)) for p in range(1, 8)
    ]
    pairs = [pl.ds(2 * q, 2) for q in range(4)]
    gather = [
        [None] + [remote(feats.at[0, pair], feats.at[d, pair], side[d]) for d in (1, 2)]
        for pair in pairs
    ]
    relay = [
        [
            None,
            remote(feats.at[2, pair, second], feats.at[3, pair, second], side[1]),
            remote(feats.at[1, pair, first], feats.at[3, pair, first], side[2]),
        ]
        for pair in pairs
    ]
    rows = [None, first, second]
    diag = [
        [None]
        + [remote(parts.at[3, pair, rows[d]], diag_in.at[d - 1, pair], side[d]) for d in (1, 2)]
        for pair in pairs
    ]
    direct = [
        [None]
        + [remote(parts.at[d, pair, rows[d]], direct_in.at[d - 1, pair], side[d]) for d in (1, 2)]
        for pair in pairs
    ]
    summed = [
        [None]
        + [remote(sum_out.at[d - 1, pair], sum_in.at[d - 1, pair], side[d]) for d in (1, 2)]
        for pair in pairs
    ]

    for p in range(1, 8):
        go(out_copies[p])
    for load in loads + cot_loads:
        load.start()

    def gather_start(q):
        for p in (2 * q, 2 * q + 1):
            if p:
                out_copies[p].wait_recv()
        go(gather[q][1])
        go(gather[q][2])

    def gather_relay(q):
        gather[q][1].wait_recv()
        go(relay[q][2])
        gather[q][2].wait_recv()
        go(relay[q][1])

    def gather_end(q):
        relay[q][1].wait_recv()
        relay[q][2].wait_recv()

    rows_all = 8 * cap

    def hidden_tile(first_block, last_block, n):
        columns = slice(n * TILE, (n + 1) * TILE)
        total = None if first_block == 0 else before_act[:, columns]
        for j in range(first_block, last_block):
            product = jnp.dot(
                feats[j].reshape(rows_all, width),
                w_v[j, :, columns],
                preferred_element_type=jnp.float32,
            )
            total = product if total is None else total + product
        if last_block < 4:
            before_act[:, columns] = total
        else:
            cotangent = cot_v[:, :, columns].reshape(rows_all, TILE).astype(jnp.float32)
            hidden[:, columns] = (cotangent * gelu_slope(total)).astype(jnp.bfloat16)

    def part_block(j):
        for n in range(width // TILE):
            columns = slice(n * TILE, (n + 1) * TILE)
            block = lax.dot_general(
                hidden[...],
                w_v[j, columns, :],
                (((1,), (1,)), ((), ())),
                preferred_element_type=jnp.float32,
            )
            parts[j, :, :, columns] = block.astype(jnp.bfloat16).reshape(8, cap, TILE)

    def sum_step(q, d):
        pair, other = pairs[q], 3 - d
        diag[q][d].wait_recv()
        sum_out[other - 1, pair] = (
            parts[other, pair, rows[d]].astype(jnp.float32)
            + diag_in[d - 1, pair].astype(jnp.float32)
        ).astype(jnp.bfloat16)
        go(summed[q][other])

    def final_step(q):
        pair = pairs[q]
        for d in (1, 2):
            direct[q][d].wait_recv()
            summed[q][3 - d].wait_recv()
            total = (
                parts[0, pair, rows[d]].astype(jnp.float32)
                + direct_in[d - 1, pair].astype(jnp.float32)
                + sum_in[2 - d, pair].astype(jnp.float32)
            ).astype(jnp.bfloat16)
            done_rows[pair, rows[d]] = total
        for p in (2 * q, 2 * q + 1):
            if p:
                go(back_copies[p])
            else:
                back_rows[0] = done_rows[0]

    tiles = ff // TILE
    gather_start(0)
    combine[...] = chosen.T.astype(jnp.bfloat16)
    gather_start(1)
    gather_relay(0)
    gather_start(2)
    gather_relay(1)
    gather_start(3)
    for load in loads + cot_loads:
        load.wait()
    hidden_tile(0, 1, 0)
    gather_relay(2)
    for n in range(1, tiles):
        hidden_tile(0, 1, n)
    gather_relay(3)
    for n in range(tiles):
        hidden_tile(1, 3, n)
    for q in range(4):
        gather_end(q)
    for n in range(tiles):
        hidden_tile(3, 4, n)
    part_block(3)
    for q in RETURN:
        go(diag[q][1])
        go(diag[q][2])
    part_block(1)
    for q in RETURN:
        sum_step(q, 2)
    part_block(2)
    for q in RETURN:
        sum_step(q, 1)
    for q in RETURN:
        go(direct[q][1])
        go(direct[q][2])
    part_block(0)
    for q in RETURN:
        final_step(q)
    for p in range(1, 8):
        back_copies[p].wait_recv()
    out_ref[...] = jnp.dot(
        combine[...],
        back_rows[...].reshape(8 * cap, width),
        preferred_element_type=jnp.float32,
    ).astype(out_ref.dtype)
    for copy in started:
        copy.wait_send()


def one_kernel(tokens, expert_ids, seq_lengths, hidden_cotangent, w_in):
    tok, width = tokens.shape
    ff = w_in.shape[2]
    cap = hidden_cotangent.shape[1] // 8
    half = cap // 2
    bf16 = jnp.bfloat16
    copies = 7 + 7 + 4 * 10
    vmem, anywhere = pl.BlockSpec(memory_space=pltpu.VMEM), pl.BlockSpec(memory_space=pl.ANY)
    smem = pl.BlockSpec(memory_space=pltpu.SMEM)
    return pl.pallas_call(
        functools.partial(kernel, cap),
        out_shape=jax.ShapeDtypeStruct((tok, width), tokens.dtype),
        in_specs=[anywhere, anywhere, smem, anywhere, anywhere],
        out_specs=vmem,
        scratch_shapes=[
            pltpu.VMEM((tok, width), bf16),
            pltpu.VMEM((1, tok), jnp.int32),
            pltpu.VMEM((4, width, ff), bf16),
            pltpu.VMEM((8, cap, ff), bf16),
            pltpu.VMEM((8, cap, width), bf16),
            pltpu.VMEM((4, 8, cap, width), bf16),
            pltpu.VMEM((4, 8, cap, width), bf16),
            pltpu.VMEM((8 * cap, ff), jnp.float32),
            pltpu.VMEM((8 * cap, ff), bf16),
            pltpu.VMEM((tok, 8 * cap), bf16),
            pltpu.VMEM((2, 8, half, width), bf16),
            pltpu.VMEM((2, 8, half, width), bf16),
            pltpu.VMEM((2, 8, half, width), bf16),
            pltpu.VMEM((2, 8, half, width), bf16),
            pltpu.VMEM((8, cap, width), bf16),
            pltpu.VMEM((8, cap, width), bf16),
            pltpu.SemaphoreType.DMA((14,)),
            pltpu.SemaphoreType.DMA((copies,)),
            pltpu.SemaphoreType.DMA((copies,)),
        ],
        compiler_params=pltpu.CompilerParams(
            collective_id=0, has_side_effects=True, vmem_limit_bytes=58 << 20
        ),
        cost_estimate=pl.CostEstimate(
            flops=4 * 8 * cap * 4 * width * ff,
            bytes_accessed=2 * 4 * width * ff,
            transcendentals=8 * cap * ff,
        ),
    )(tokens, expert_ids.reshape(1, tok), seq_lengths, hidden_cotangent, w_in)


def solution(mesh):
    in_specs = (
        P("expert", "mp"),
        P("expert", None),
        P("expert"),
        P("expert", None, "mp"),
        P("expert", None, "mp"),
    )
    out_specs = P("expert", "mp")
    small = mesh.shape["mp"] == 4 and mesh.shape["expert"] == 8
    return jax.shard_map(
        one_kernel if small else per_device,
        mesh=mesh,
        in_specs=in_specs,
        out_specs=out_specs,
        check_vma=False,
    )
```

```python
import functools
import math

import jax
import jax.numpy as jnp
from jax import lax
from jax.experimental import pallas as pl
from jax.experimental.pallas import tpu as pltpu
from jax.sharding import PartitionSpec as P

SEQ_LEN = 128
MESH = pl.DeviceIdType.MESH
ORDER = (0, 1, 4, 5, 6, 7, 2, 3)
TILE = 512
def gelu_slope(preact):
    coeff = math.sqrt(2.0 / math.pi)
    squashed = jnp.tanh(coeff * (preact + 0.044715 * preact * preact * preact))
    return 0.5 * (1.0 + squashed) + 0.5 * preact * (1.0 - squashed * squashed) * coeff * (
        1.0 + 3.0 * 0.044715 * preact * preact
    )


def per_device(tokens, expert_ids, seq_lengths, hidden_cotangent, w_in):
    tok_dev = tokens.shape[0]
    experts = w_in.shape[0] * lax.axis_size("expert")
    capacity = max(2, 2 * tok_dev // experts)
    position = jnp.arange(tok_dev, dtype=jnp.int32)
    seq_index = position // SEQ_LEN
    seq_length = jnp.sum(
        jnp.where(
            seq_index[:, None] == jnp.arange(seq_lengths.shape[0], dtype=jnp.int32)[None, :],
            seq_lengths[None, :],
            0,
        ),
        axis=1,
    )
    live_mask = position % SEQ_LEN < seq_length
    expert_row = expert_ids[:, 0]
    onehot = (
        (expert_row[:, None] == jnp.arange(experts, dtype=jnp.int32)[None, :]) & live_mask[:, None]
    ).astype(jnp.int32)
    slot_rank = jnp.sum(jnp.cumsum(onehot, axis=0) * onehot, axis=1) - 1
    target = jnp.where(live_mask, expert_row * capacity + slot_rank, experts * capacity)
    buffer = (
        jnp.zeros((experts * capacity + 1,) + tokens.shape[1:], tokens.dtype).at[target].set(tokens)
    )
    arrived = lax.all_to_all(
        buffer[:-1].reshape((experts, capacity) + tokens.shape[1:]),
        "expert",
        split_axis=0,
        concat_axis=0,
        tiled=True,
    )
    slot_count = arrived.shape[0] * capacity
    features = lax.all_gather(
        arrived.reshape(slot_count, arrived.shape[2]), "mp", axis=1, tiled=True
    )
    weight = w_in[0]
    pre_act = jnp.dot(features, weight, preferred_element_type=jnp.float32)
    hidden_grad = (hidden_cotangent[0].astype(jnp.float32) * gelu_slope(pre_act)).astype(
        jnp.bfloat16
    )
    partial_value = lax.dot_general(
        hidden_grad, weight, (((1,), (1,)), ((), ())), preferred_element_type=jnp.float32
    ).astype(jnp.bfloat16)
    partial_value = lax.optimization_barrier(partial_value)
    summed = lax.psum_scatter(
        partial_value.astype(jnp.float32).astype(jnp.bfloat16),
        "mp",
        scatter_dimension=1,
        tiled=True,
    )
    returned = lax.all_to_all(
        summed.reshape(arrived.shape[0], capacity, summed.shape[1]),
        "expert",
        split_axis=0,
        concat_axis=0,
        tiled=True,
    )
    flat_rows = returned.reshape((experts * capacity,) + returned.shape[2:])
    padded = jnp.concatenate(
        [flat_rows, jnp.zeros((1,) + flat_rows.shape[1:], flat_rows.dtype)], axis=0
    )
    return padded[target]


def flip(index, difference, bits):
    total = 0
    for bit in range(bits):
        value = lax.rem(index // (1 << bit), 2)
        total = total + (1 << bit) * ((1 - value) if difference >> bit & 1 else value)
    return total


def kernel(
    cap,
    tokens_hbm,
    ids_hbm,
    lengths_ref,
    cot_hbm,
    w_hbm,
    out_ref,
    tokens_ref,
    ids_ref,
    w_v,
    cot_v,
    send_rows,
    feats,
    parts,
    hidden,
    combine,
    diag_in,
    direct_in,
    sum_in,
    sum_out,
    done_rows,
    back_rows,
    local_sem,
    send_sem,
    recv_sem,
):
    expert, place = lax.axis_index("expert"), lax.axis_index("mp")
    peers = [flip(expert, k, 3) for k in ORDER]
    side = [None, (expert, flip(place, 1, 2)), (expert, flip(place, 2, 2))]
    tok, width = tokens_ref.shape
    ff = w_v.shape[2]
    half = cap // 2
    first, second = pl.ds(0, half), pl.ds(half, half)

    barrier = pltpu.get_barrier_semaphore()
    greeted = [(peer, place) for peer in peers[1:]] + side[1:]
    for device in greeted:
        pl.semaphore_signal(barrier, inc=1, device_id=device, device_id_type=MESH)

    inputs = [
        pltpu.make_async_copy(source, target, local_sem.at[12 + n])
        for n, (source, target) in enumerate(
            ((ids_hbm, ids_ref), (tokens_hbm, tokens_ref))
        )
    ]
    for load in inputs:
        load.start()
    loads = []
    for j in range(4):
        start = pl.multiple_of(flip(place, j, 2) * width, width)
        loads.append(
            pltpu.make_async_copy(w_hbm.at[0, pl.ds(start, width)], w_v.at[j], local_sem.at[j])
        )
    cot_loads = []
    for p in range(8):
        start = pl.multiple_of(peers[p] * cap, cap)
        cot_loads.append(
            pltpu.make_async_copy(
                cot_hbm.at[0, pl.ds(start, cap)], cot_v.at[p], local_sem.at[4 + p]
            )
        )

    position = lax.broadcasted_iota(jnp.int32, (1, tok), 1)
    limit = jnp.zeros((1, tok), jnp.int32)
    inputs[0].wait()
    for i in range(lengths_ref.shape[0]):
        limit = jnp.where(position // SEQ_LEN == i, lengths_ref[i], limit)
    live = position % SEQ_LEN < limit
    away = jnp.bitwise_xor(ids_ref[...], expert)
    rank_of = jnp.zeros((1, tok), jnp.int32)
    for p, k in enumerate(ORDER):
        rank_of = jnp.where(away == k, p, rank_of)
    rank_of = jnp.where(live, rank_of, -1)
    onehot = jnp.where(
        lax.broadcasted_iota(jnp.int32, (16, tok), 0) == rank_of, 1.0, 0.0
    )
    before = lax.broadcasted_iota(jnp.int32, (tok, tok), 0) <= lax.broadcasted_iota(
        jnp.int32, (tok, tok), 1
    )
    counts = jnp.dot(
        onehot.astype(jnp.bfloat16),
        jnp.where(before, 1.0, 0.0).astype(jnp.bfloat16),
        preferred_element_type=jnp.float32,
    )
    slot = jnp.sum(counts * onehot, axis=0, keepdims=True) - 1.0
    slot = jnp.where(live, slot + (rank_of * cap).astype(jnp.float32), -1.0)
    slots = lax.broadcasted_iota(jnp.int32, (8 * cap, tok), 0).astype(jnp.float32)
    chosen = jnp.where(slots == slot, 1.0, 0.0)
    inputs[1].wait()
    placed = jnp.dot(
        chosen.astype(jnp.bfloat16), tokens_ref[...], preferred_element_type=jnp.float32
    ).astype(jnp.bfloat16)
    feats[0, 0] = placed[:cap]
    for p in range(1, 8):
        send_rows[p] = placed[p * cap : (p + 1) * cap]

    pl.semaphore_wait(barrier, len(greeted))

    started = []
    numbers = iter(range(1000))

    def remote(source, target, device):
        n = next(numbers)
        return pltpu.make_async_remote_copy(
            src_ref=source,
            dst_ref=target,
            send_sem=send_sem.at[n],
            recv_sem=recv_sem.at[n],
            device_id=device,
            device_id_type=MESH,
        )

    def go(copy):
        copy.start()
        started.append(copy)

    out_copies = [None] + [
        remote(send_rows.at[p], feats.at[0, p], (peers[p], place)) for p in range(1, 8)
    ]
    back_copies = [None] + [
        remote(done_rows.at[p], back_rows.at[p], (peers[p], place)) for p in range(1, 8)
    ]
    pairs = [pl.ds(2 * q, 2) for q in range(4)]
    gather = [
        [None] + [remote(feats.at[0, pair], feats.at[d, pair], side[d]) for d in (1, 2)]
        for pair in pairs[1:]
    ]
    gather = [None] + gather
    relay = [
        [
            None,
            remote(feats.at[2, pair, second], feats.at[3, pair, second], side[1]),
            remote(feats.at[1, pair, first], feats.at[3, pair, first], side[2]),
        ]
        for pair in pairs
    ]
    rows = [None, first, second]
    diag = [
        [None]
        + [remote(parts.at[3, pair, rows[d]], diag_in.at[d - 1, pair], side[d]) for d in (1, 2)]
        for pair in pairs
    ]
    direct = [
        [None]
        + [remote(parts.at[d, pair, rows[d]], direct_in.at[d - 1, pair], side[d]) for d in (1, 2)]
        for pair in pairs
    ]
    summed = [
        [None]
        + [remote(sum_out.at[d - 1, pair], sum_in.at[d - 1, pair], side[d]) for d in (1, 2)]
        for pair in pairs
    ]

    own = [None] + [remote(feats.at[0, 0], feats.at[d, 0], side[d]) for d in (1, 2)]
    peer = [None] + [remote(feats.at[0, 1], feats.at[d, 1], side[d]) for d in (1, 2)]
    go(own[1])
    go(own[2])
    for p in range(1, 8):
        go(out_copies[p])
    for load in loads + cot_loads:
        load.start()

    def gather_start(q):
        if q == 0:
            out_copies[1].wait_recv()
            go(peer[1])
            go(peer[2])
            return
        out_copies[2 * q].wait_recv()
        out_copies[2 * q + 1].wait_recv()
        go(gather[q][1])
        go(gather[q][2])

    def gather_relay(q):
        for d in (1, 2):
            if q == 0:
                own[d].wait_recv()
                peer[d].wait_recv()
            else:
                gather[q][d].wait_recv()
            go(relay[q][3 - d])

    def gather_end(q):
        relay[q][1].wait_recv()
        relay[q][2].wait_recv()

    rows_all = 4 * cap

    def hidden_tile(g, n):
        group, columns = slice(4 * g, 4 * g + 4), slice(n * TILE, (n + 1) * TILE)
        total = None
        for j in range(4):
            product = jnp.dot(
                feats[j, group].reshape(rows_all, width),
                w_v[j, :, columns],
                preferred_element_type=jnp.float32,
            )
            total = product if total is None else total + product
        cotangent = cot_v[group, :, columns].reshape(rows_all, TILE).astype(jnp.float32)
        hidden[:, columns] = (cotangent * gelu_slope(total)).astype(jnp.bfloat16)

    def part_block(g, j):
        group = slice(4 * g, 4 * g + 4)
        for n in range(width // TILE):
            columns = slice(n * TILE, (n + 1) * TILE)
            block = lax.dot_general(
                hidden[...],
                w_v[j, columns, :],
                (((1,), (1,)), ((), ())),
                preferred_element_type=jnp.float32,
            )
            parts[j, group, :, columns] = block.astype(jnp.bfloat16).reshape(4, cap, TILE)

    def sum_step(q, d):
        pair, other = pairs[q], 3 - d
        diag[q][d].wait_recv()
        sum_out[other - 1, pair] = (
            parts[other, pair, rows[d]].astype(jnp.float32)
            + diag_in[d - 1, pair].astype(jnp.float32)
        ).astype(jnp.bfloat16)
        go(summed[q][other])

    def final_step(q):
        pair = pairs[q]
        for d in (1, 2):
            direct[q][d].wait_recv()
            summed[q][3 - d].wait_recv()
            total = (
                parts[0, pair, rows[d]].astype(jnp.float32)
                + direct_in[d - 1, pair].astype(jnp.float32)
                + sum_in[2 - d, pair].astype(jnp.float32)
            ).astype(jnp.bfloat16)
            done_rows[pair, rows[d]] = total
        for p in (2 * q, 2 * q + 1):
            if p:
                go(back_copies[p])
            else:
                back_rows[0] = done_rows[0]

    tiles = ff // TILE
    gather_start(0)
    combine[...] = chosen.T.astype(jnp.bfloat16)
    gather_relay(0)
    gather_start(1)
    gather_relay(1)
    for load in loads + cot_loads:
        load.wait()
    gather_end(0)
    gather_end(1)
    hidden_tile(0, 0)
    gather_start(2)
    for n in range(1, tiles):
        hidden_tile(0, n)
    gather_start(3)
    part_block(0, 3)
    for q in (0, 1):
        go(diag[q][1])
        go(diag[q][2])
    gather_relay(2)
    part_block(0, 1)
    sum_step(0, 2)
    gather_relay(3)
    sum_step(1, 2)
    part_block(0, 2)
    sum_step(0, 1)
    sum_step(1, 1)
    for q in (0, 1):
        go(direct[q][1])
        go(direct[q][2])
    part_block(0, 0)
    gather_end(2)
    gather_end(3)
    hidden_tile(1, 0)
    for n in range(1, tiles):
        hidden_tile(1, n)
    part_block(1, 3)
    for q in (2, 3):
        go(diag[q][1])
        go(diag[q][2])
    final_step(1)
    part_block(1, 1)
    sum_step(2, 2)
    sum_step(3, 2)
    part_block(1, 2)
    sum_step(2, 1)
    sum_step(3, 1)
    for q in (2, 3):
        go(direct[q][1])
        go(direct[q][2])
    final_step(0)
    part_block(1, 0)
    final_step(2)
    final_step(3)
    for p in range(1, 8):
        back_copies[p].wait_recv()
    out_ref[...] = jnp.dot(
        combine[...],
        back_rows[...].reshape(8 * cap, width),
        preferred_element_type=jnp.float32,
    ).astype(out_ref.dtype)
    for copy in started:
        copy.wait_send()


def one_kernel(tokens, expert_ids, seq_lengths, hidden_cotangent, w_in):
    tok, width = tokens.shape
    ff = w_in.shape[2]
    cap = hidden_cotangent.shape[1] // 8
    half = cap // 2
    bf16 = jnp.bfloat16
    copies = 7 + 7 + 4 * 10 + 2
    vmem, anywhere = pl.BlockSpec(memory_space=pltpu.VMEM), pl.BlockSpec(memory_space=pl.ANY)
    smem = pl.BlockSpec(memory_space=pltpu.SMEM)
    return pl.pallas_call(
        functools.partial(kernel, cap),
        out_shape=jax.ShapeDtypeStruct((tok, width), tokens.dtype),
        in_specs=[anywhere, anywhere, smem, anywhere, anywhere],
        out_specs=vmem,
        scratch_shapes=[
            pltpu.VMEM((tok, width), bf16),
            pltpu.VMEM((1, tok), jnp.int32),
            pltpu.VMEM((4, width, ff), bf16),
            pltpu.VMEM((8, cap, ff), bf16),
            pltpu.VMEM((8, cap, width), bf16),
            pltpu.VMEM((4, 8, cap, width), bf16),
            pltpu.VMEM((4, 8, cap, width), bf16),
            pltpu.VMEM((4 * cap, ff), bf16),
            pltpu.VMEM((tok, 8 * cap), bf16),
            pltpu.VMEM((2, 8, half, width), bf16),
            pltpu.VMEM((2, 8, half, width), bf16),
            pltpu.VMEM((2, 8, half, width), bf16),
            pltpu.VMEM((2, 8, half, width), bf16),
            pltpu.VMEM((8, cap, width), bf16),
            pltpu.VMEM((8, cap, width), bf16),
            pltpu.SemaphoreType.DMA((14,)),
            pltpu.SemaphoreType.DMA((copies,)),
            pltpu.SemaphoreType.DMA((copies,)),
        ],
        compiler_params=pltpu.CompilerParams(
            collective_id=0, has_side_effects=True, vmem_limit_bytes=58 << 20
        ),
        cost_estimate=pl.CostEstimate(
            flops=4 * 8 * cap * 4 * width * ff,
            bytes_accessed=2 * 4 * width * ff,
            transcendentals=8 * cap * ff,
        ),
    )(tokens, expert_ids.reshape(1, tok), seq_lengths, hidden_cotangent, w_in)


def solution(mesh):
    in_specs = (
        P("expert", "mp"),
        P("expert", None),
        P("expert"),
        P("expert", None, "mp"),
        P("expert", None, "mp"),
    )
    out_specs = P("expert", "mp")
    small = mesh.shape["mp"] == 4 and mesh.shape["expert"] == 8
    return jax.shard_map(
        one_kernel if small else per_device,
        mesh=mesh,
        in_specs=in_specs,
        out_specs=out_specs,
        check_vma=False,
    )
```

```python
import functools
import math

import jax
import jax.numpy as jnp
from jax import lax
from jax.experimental import pallas as pl
from jax.experimental.pallas import tpu as pltpu
from jax.sharding import PartitionSpec as P

SEQ_LEN = 128
MESH = pl.DeviceIdType.MESH
ORDER = (0, 1, 4, 5, 2, 3, 6, 7)
RETURN = (3, 1, 2, 0)
TILE = 512
def gelu_slope(preact):
    coeff = math.sqrt(2.0 / math.pi)
    squashed = jnp.tanh(coeff * (preact + 0.044715 * preact * preact * preact))
    return 0.5 * (1.0 + squashed) + 0.5 * preact * (1.0 - squashed * squashed) * coeff * (
        1.0 + 3.0 * 0.044715 * preact * preact
    )


def per_device(tokens, expert_ids, seq_lengths, hidden_cotangent, w_in):
    tok_dev = tokens.shape[0]
    experts = w_in.shape[0] * lax.axis_size("expert")
    capacity = max(2, 2 * tok_dev // experts)
    position = jnp.arange(tok_dev, dtype=jnp.int32)
    seq_index = position // SEQ_LEN
    seq_length = jnp.sum(
        jnp.where(
            seq_index[:, None] == jnp.arange(seq_lengths.shape[0], dtype=jnp.int32)[None, :],
            seq_lengths[None, :],
            0,
        ),
        axis=1,
    )
    live_mask = position % SEQ_LEN < seq_length
    expert_row = expert_ids[:, 0]
    onehot = (
        (expert_row[:, None] == jnp.arange(experts, dtype=jnp.int32)[None, :]) & live_mask[:, None]
    ).astype(jnp.int32)
    slot_rank = jnp.sum(jnp.cumsum(onehot, axis=0) * onehot, axis=1) - 1
    target = jnp.where(live_mask, expert_row * capacity + slot_rank, experts * capacity)
    buffer = (
        jnp.zeros((experts * capacity + 1,) + tokens.shape[1:], tokens.dtype).at[target].set(tokens)
    )
    arrived = lax.all_to_all(
        buffer[:-1].reshape((experts, capacity) + tokens.shape[1:]),
        "expert",
        split_axis=0,
        concat_axis=0,
        tiled=True,
    )
    slot_count = arrived.shape[0] * capacity
    features = lax.all_gather(
        arrived.reshape(slot_count, arrived.shape[2]), "mp", axis=1, tiled=True
    )
    weight = w_in[0]
    pre_act = jnp.dot(features, weight, preferred_element_type=jnp.float32)
    hidden_grad = (hidden_cotangent[0].astype(jnp.float32) * gelu_slope(pre_act)).astype(
        jnp.bfloat16
    )
    partial_value = lax.dot_general(
        hidden_grad, weight, (((1,), (1,)), ((), ())), preferred_element_type=jnp.float32
    ).astype(jnp.bfloat16)
    partial_value = lax.optimization_barrier(partial_value)
    summed = lax.psum_scatter(
        partial_value.astype(jnp.float32).astype(jnp.bfloat16),
        "mp",
        scatter_dimension=1,
        tiled=True,
    )
    returned = lax.all_to_all(
        summed.reshape(arrived.shape[0], capacity, summed.shape[1]),
        "expert",
        split_axis=0,
        concat_axis=0,
        tiled=True,
    )
    flat_rows = returned.reshape((experts * capacity,) + returned.shape[2:])
    padded = jnp.concatenate(
        [flat_rows, jnp.zeros((1,) + flat_rows.shape[1:], flat_rows.dtype)], axis=0
    )
    return padded[target]


def flip(index, difference, bits):
    total = 0
    for bit in range(bits):
        value = lax.rem(index // (1 << bit), 2)
        total = total + (1 << bit) * ((1 - value) if difference >> bit & 1 else value)
    return total


def kernel(
    cap,
    tokens_hbm,
    ids_hbm,
    lengths_ref,
    cot_hbm,
    w_hbm,
    out_ref,
    tokens_ref,
    ids_ref,
    w_v,
    cot_v,
    send_rows,
    feats,
    parts,
    before_act,
    hidden,
    combine,
    diag_in,
    direct_in,
    sum_in,
    sum_out,
    done_rows,
    back_rows,
    local_sem,
    send_sem,
    recv_sem,
):
    expert, place = lax.axis_index("expert"), lax.axis_index("mp")
    peers = [flip(expert, k, 3) for k in ORDER]
    side = [None, (expert, flip(place, 1, 2)), (expert, flip(place, 2, 2))]
    tok, width = tokens_ref.shape
    ff = w_v.shape[2]
    half = cap // 2
    first, second = pl.ds(0, half), pl.ds(half, half)

    barrier = pltpu.get_barrier_semaphore()
    greeted = [(peer, place) for peer in peers[1:]] + side[1:]
    for device in greeted:
        pl.semaphore_signal(barrier, inc=1, device_id=device, device_id_type=MESH)

    inputs = [
        pltpu.make_async_copy(source, target, local_sem.at[12 + n])
        for n, (source, target) in enumerate(
            ((ids_hbm, ids_ref), (tokens_hbm, tokens_ref))
        )
    ]
    for load in inputs:
        load.start()
    loads = []
    for j in range(4):
        start = pl.multiple_of(flip(place, j, 2) * width, width)
        loads.append(
            pltpu.make_async_copy(w_hbm.at[0, pl.ds(start, width)], w_v.at[j], local_sem.at[j])
        )
    cot_loads = []
    for p in range(8):
        start = pl.multiple_of(peers[p] * cap, cap)
        cot_loads.append(
            pltpu.make_async_copy(
                cot_hbm.at[0, pl.ds(start, cap)], cot_v.at[p], local_sem.at[4 + p]
            )
        )

    position = lax.broadcasted_iota(jnp.int32, (1, tok), 1)
    limit = jnp.zeros((1, tok), jnp.int32)
    inputs[0].wait()
    for i in range(lengths_ref.shape[0]):
        limit = jnp.where(position // SEQ_LEN == i, lengths_ref[i], limit)
    live = position % SEQ_LEN < limit
    away = jnp.bitwise_xor(ids_ref[...], expert)
    rank_of = jnp.zeros((1, tok), jnp.int32)
    for p, k in enumerate(ORDER):
        rank_of = jnp.where(away == k, p, rank_of)
    rank_of = jnp.where(live, rank_of, -1)
    onehot = jnp.where(
        lax.broadcasted_iota(jnp.int32, (16, tok), 0) == rank_of, 1.0, 0.0
    )
    before = lax.broadcasted_iota(jnp.int32, (tok, tok), 0) <= lax.broadcasted_iota(
        jnp.int32, (tok, tok), 1
    )
    counts = jnp.dot(
        onehot.astype(jnp.bfloat16),
        jnp.where(before, 1.0, 0.0).astype(jnp.bfloat16),
        preferred_element_type=jnp.float32,
    )
    slot = jnp.sum(counts * onehot, axis=0, keepdims=True) - 1.0
    slot = jnp.where(live, slot + (rank_of * cap).astype(jnp.float32), -1.0)
    slots = lax.broadcasted_iota(jnp.int32, (8 * cap, tok), 0).astype(jnp.float32)
    chosen = jnp.where(slots == slot, 1.0, 0.0)
    inputs[1].wait()
    placed = jnp.dot(
        chosen.astype(jnp.bfloat16), tokens_ref[...], preferred_element_type=jnp.float32
    ).astype(jnp.bfloat16)
    feats[0, 0] = placed[:cap]
    for p in range(1, 8):
        send_rows[p] = placed[p * cap : (p + 1) * cap]

    pl.semaphore_wait(barrier, len(greeted))

    started = []
    numbers = iter(range(1000))

    def remote(source, target, device):
        n = next(numbers)
        return pltpu.make_async_remote_copy(
            src_ref=source,
            dst_ref=target,
            send_sem=send_sem.at[n],
            recv_sem=recv_sem.at[n],
            device_id=device,
            device_id_type=MESH,
        )

    def go(copy):
        copy.start()
        started.append(copy)

    out_copies = [None] + [
        remote(send_rows.at[p], feats.at[0, p], (peers[p], place)) for p in range(1, 8)
    ]
    back_copies = [None] + [
        remote(done_rows.at[p], back_rows.at[p], (peers[p], place)) for p in range(1, 8)
    ]
    pairs = [pl.ds(2 * q, 2) for q in range(4)]
    gather = [
        [None] + [remote(feats.at[0, pair], feats.at[d, pair], side[d]) for d in (1, 2)]
        for pair in pairs[1:]
    ]
    gather = [None] + gather
    relay = [
        [
            None,
            remote(feats.at[2, pair, second], feats.at[3, pair, second], side[1]),
            remote(feats.at[1, pair, first], feats.at[3, pair, first], side[2]),
        ]
        for pair in pairs
    ]
    rows = [None, first, second]
    diag = [
        [None]
        + [remote(parts.at[3, pair, rows[d]], diag_in.at[d - 1, pair], side[d]) for d in (1, 2)]
        for pair in pairs
    ]
    direct = [
        [None]
        + [remote(parts.at[d, pair, rows[d]], direct_in.at[d - 1, pair], side[d]) for d in (1, 2)]
        for pair in pairs
    ]
    summed = [
        [None]
        + [remote(sum_out.at[d - 1, pair], sum_in.at[d - 1, pair], side[d]) for d in (1, 2)]
        for pair in pairs
    ]

    own = [None] + [remote(feats.at[0, 0], feats.at[d, 0], side[d]) for d in (1, 2)]
    peer = [None] + [remote(feats.at[0, 1], feats.at[d, 1], side[d]) for d in (1, 2)]
    go(own[1])
    go(own[2])
    for p in (1, 2, 3):
        go(out_copies[p])
    for load in loads + cot_loads:
        load.start()

    def gather_start(q):
        if q == 0:
            out_copies[1].wait_recv()
            go(peer[1])
            go(peer[2])
            return
        out_copies[2 * q].wait_recv()
        out_copies[2 * q + 1].wait_recv()
        go(gather[q][1])
        go(gather[q][2])

    def gather_relay(q):
        for d in (1, 2):
            if q == 0:
                own[d].wait_recv()
                peer[d].wait_recv()
            else:
                gather[q][d].wait_recv()
            go(relay[q][3 - d])

    def gather_end(q):
        relay[q][1].wait_recv()
        relay[q][2].wait_recv()

    rows_all = 8 * cap

    def hidden_tile(first_block, last_block, n):
        columns = slice(n * TILE, (n + 1) * TILE)
        total = None if first_block == 0 else before_act[:, columns]
        for j in range(first_block, last_block):
            product = jnp.dot(
                feats[j].reshape(rows_all, width),
                w_v[j, :, columns],
                preferred_element_type=jnp.float32,
            )
            total = product if total is None else total + product
        if last_block < 4:
            before_act[:, columns] = total
        else:
            cotangent = cot_v[:, :, columns].reshape(rows_all, TILE).astype(jnp.float32)
            hidden[:, columns] = (cotangent * gelu_slope(total)).astype(jnp.bfloat16)

    def part_block(j):
        for n in range(width // TILE):
            columns = slice(n * TILE, (n + 1) * TILE)
            block = lax.dot_general(
                w_v[j, columns, :],
                hidden[...],
                (((1,), (1,)), ((), ())),
                preferred_element_type=jnp.float32,
            )
            parts[j, :, :, columns] = block.T.astype(jnp.bfloat16).reshape(8, cap, TILE)

    def sum_step(q, d):
        pair, other = pairs[q], 3 - d
        diag[q][d].wait_recv()
        sum_out[other - 1, pair] = (
            parts[other, pair, rows[d]].astype(jnp.float32)
            + diag_in[d - 1, pair].astype(jnp.float32)
        ).astype(jnp.bfloat16)
        go(summed[q][other])

    def final_step(q):
        pair = pairs[q]
        for d in (1, 2):
            direct[q][d].wait_recv()
            summed[q][3 - d].wait_recv()
            total = (
                parts[0, pair, rows[d]].astype(jnp.float32)
                + direct_in[d - 1, pair].astype(jnp.float32)
                + sum_in[2 - d, pair].astype(jnp.float32)
            ).astype(jnp.bfloat16)
            done_rows[pair, rows[d]] = total
        for p in (2 * q, 2 * q + 1):
            if p:
                go(back_copies[p])
            else:
                back_rows[0] = done_rows[0]

    tiles = ff // TILE
    gather_start(0)
    combine[...] = chosen.T.astype(jnp.bfloat16)
    gather_relay(0)
    gather_start(1)
    for p in (6, 7, 4, 5):
        go(out_copies[p])
    gather_relay(1)
    gather_start(2)
    gather_relay(2)
    gather_start(3)
    for load in loads + cot_loads:
        load.wait()
    for n in range(tiles):
        hidden_tile(0, 1, n)
    gather_relay(3)
    for n in range(tiles):
        hidden_tile(1, 3, n)
    for q in range(4):
        gather_end(q)
    for n in range(tiles):
        hidden_tile(3, 4, n)
    part_block(3)
    for q in RETURN:
        go(diag[q][1])
        go(diag[q][2])
    for j in (1, 2, 0):
        part_block(j)
    for q in RETURN:
        sum_step(q, 2)
        sum_step(q, 1)
        go(direct[q][1])
        go(direct[q][2])
    for q in RETURN:
        final_step(q)
    for p in range(1, 8):
        back_copies[p].wait_recv()
    out_ref[...] = jnp.dot(
        combine[...],
        back_rows[...].reshape(8 * cap, width),
        preferred_element_type=jnp.float32,
    ).astype(out_ref.dtype)
    for copy in started:
        copy.wait_send()


def one_kernel(tokens, expert_ids, seq_lengths, hidden_cotangent, w_in):
    tok, width = tokens.shape
    ff = w_in.shape[2]
    cap = hidden_cotangent.shape[1] // 8
    half = cap // 2
    bf16 = jnp.bfloat16
    copies = 7 + 7 + 4 * 10 + 2
    vmem, anywhere = pl.BlockSpec(memory_space=pltpu.VMEM), pl.BlockSpec(memory_space=pl.ANY)
    smem = pl.BlockSpec(memory_space=pltpu.SMEM)
    return pl.pallas_call(
        functools.partial(kernel, cap),
        out_shape=jax.ShapeDtypeStruct((tok, width), tokens.dtype),
        in_specs=[anywhere, anywhere, smem, anywhere, anywhere],
        out_specs=vmem,
        scratch_shapes=[
            pltpu.VMEM((tok, width), bf16),
            pltpu.VMEM((1, tok), jnp.int32),
            pltpu.VMEM((4, width, ff), bf16),
            pltpu.VMEM((8, cap, ff), bf16),
            pltpu.VMEM((8, cap, width), bf16),
            pltpu.VMEM((4, 8, cap, width), bf16),
            pltpu.VMEM((4, 8, cap, width), bf16),
            pltpu.VMEM((8 * cap, ff), jnp.float32),
            pltpu.VMEM((8 * cap, ff), bf16),
            pltpu.VMEM((tok, 8 * cap), bf16),
            pltpu.VMEM((2, 8, half, width), bf16),
            pltpu.VMEM((2, 8, half, width), bf16),
            pltpu.VMEM((2, 8, half, width), bf16),
            pltpu.VMEM((2, 8, half, width), bf16),
            pltpu.VMEM((8, cap, width), bf16),
            pltpu.VMEM((8, cap, width), bf16),
            pltpu.SemaphoreType.DMA((14,)),
            pltpu.SemaphoreType.DMA((copies,)),
            pltpu.SemaphoreType.DMA((copies,)),
        ],
        compiler_params=pltpu.CompilerParams(
            collective_id=0, has_side_effects=True, vmem_limit_bytes=58 << 20
        ),
        cost_estimate=pl.CostEstimate(
            flops=4 * 8 * cap * 4 * width * ff,
            bytes_accessed=2 * 4 * width * ff,
            transcendentals=8 * cap * ff,
        ),
    )(tokens, expert_ids.reshape(1, tok), seq_lengths, hidden_cotangent, w_in)


def solution(mesh):
    in_specs = (
        P("expert", "mp"),
        P("expert", None),
        P("expert"),
        P("expert", None, "mp"),
        P("expert", None, "mp"),
    )
    out_specs = P("expert", "mp")
    small = mesh.shape["mp"] == 4 and mesh.shape["expert"] == 8
    return jax.shard_map(
        one_kernel if small else per_device,
        mesh=mesh,
        in_specs=in_specs,
        out_specs=out_specs,
        check_vma=False,
    )
```

```python
import functools
import math

import jax
import jax.numpy as jnp
from jax import lax
from jax.experimental import pallas as pl
from jax.experimental.pallas import tpu as pltpu
from jax.sharding import PartitionSpec as P

SEQ_LEN = 128
MESH = pl.DeviceIdType.MESH
ORDER = (0, 1, 4, 5, 2, 3, 6, 7)
RETURN = (3, 2, 1, 0)
TILE = 512
def gelu_slope(preact):
    coeff = math.sqrt(2.0 / math.pi)
    squashed = jnp.tanh(coeff * (preact + 0.044715 * preact * preact * preact))
    return 0.5 * (1.0 + squashed) + 0.5 * preact * (1.0 - squashed * squashed) * coeff * (
        1.0 + 3.0 * 0.044715 * preact * preact
    )


def per_device(tokens, expert_ids, seq_lengths, hidden_cotangent, w_in):
    tok_dev = tokens.shape[0]
    experts = w_in.shape[0] * lax.axis_size("expert")
    capacity = max(2, 2 * tok_dev // experts)
    position = jnp.arange(tok_dev, dtype=jnp.int32)
    seq_index = position // SEQ_LEN
    seq_length = jnp.sum(
        jnp.where(
            seq_index[:, None] == jnp.arange(seq_lengths.shape[0], dtype=jnp.int32)[None, :],
            seq_lengths[None, :],
            0,
        ),
        axis=1,
    )
    live_mask = position % SEQ_LEN < seq_length
    expert_row = expert_ids[:, 0]
    onehot = (
        (expert_row[:, None] == jnp.arange(experts, dtype=jnp.int32)[None, :]) & live_mask[:, None]
    ).astype(jnp.int32)
    slot_rank = jnp.sum(jnp.cumsum(onehot, axis=0) * onehot, axis=1) - 1
    target = jnp.where(live_mask, expert_row * capacity + slot_rank, experts * capacity)
    buffer = (
        jnp.zeros((experts * capacity + 1,) + tokens.shape[1:], tokens.dtype).at[target].set(tokens)
    )
    arrived = lax.all_to_all(
        buffer[:-1].reshape((experts, capacity) + tokens.shape[1:]),
        "expert",
        split_axis=0,
        concat_axis=0,
        tiled=True,
    )
    slot_count = arrived.shape[0] * capacity
    features = lax.all_gather(
        arrived.reshape(slot_count, arrived.shape[2]), "mp", axis=1, tiled=True
    )
    weight = w_in[0]
    pre_act = jnp.dot(features, weight, preferred_element_type=jnp.float32)
    hidden_grad = (hidden_cotangent[0].astype(jnp.float32) * gelu_slope(pre_act)).astype(
        jnp.bfloat16
    )
    partial_value = lax.dot_general(
        hidden_grad, weight, (((1,), (1,)), ((), ())), preferred_element_type=jnp.float32
    ).astype(jnp.bfloat16)
    partial_value = lax.optimization_barrier(partial_value)
    summed = lax.psum_scatter(
        partial_value.astype(jnp.float32).astype(jnp.bfloat16),
        "mp",
        scatter_dimension=1,
        tiled=True,
    )
    returned = lax.all_to_all(
        summed.reshape(arrived.shape[0], capacity, summed.shape[1]),
        "expert",
        split_axis=0,
        concat_axis=0,
        tiled=True,
    )
    flat_rows = returned.reshape((experts * capacity,) + returned.shape[2:])
    padded = jnp.concatenate(
        [flat_rows, jnp.zeros((1,) + flat_rows.shape[1:], flat_rows.dtype)], axis=0
    )
    return padded[target]


def flip(index, difference, bits):
    total = 0
    for bit in range(bits):
        value = lax.rem(index // (1 << bit), 2)
        total = total + (1 << bit) * ((1 - value) if difference >> bit & 1 else value)
    return total


def kernel(
    cap,
    tokens_hbm,
    ids_hbm,
    lengths_ref,
    cot_hbm,
    w_hbm,
    out_ref,
    tokens_ref,
    ids_ref,
    w_v,
    cot_v,
    send_rows,
    feats,
    parts,
    hidden,
    combine,
    diag_in,
    direct_in,
    sum_in,
    sum_out,
    done_rows,
    back_rows,
    local_sem,
    send_sem,
    recv_sem,
):
    expert, place = lax.axis_index("expert"), lax.axis_index("mp")
    peers = [flip(expert, k, 3) for k in ORDER]
    side = [None, (expert, flip(place, 1, 2)), (expert, flip(place, 2, 2))]
    tok, width = tokens_ref.shape
    ff = w_v.shape[2]
    half = cap // 2
    first, second = pl.ds(0, half), pl.ds(half, half)

    barrier = pltpu.get_barrier_semaphore()
    greeted = [(peer, place) for peer in peers[1:]] + side[1:]
    for device in greeted:
        pl.semaphore_signal(barrier, inc=1, device_id=device, device_id_type=MESH)

    inputs = [
        pltpu.make_async_copy(source, target, local_sem.at[12 + n])
        for n, (source, target) in enumerate(
            ((ids_hbm, ids_ref), (tokens_hbm, tokens_ref))
        )
    ]
    for load in inputs:
        load.start()
    loads = []
    for j in range(4):
        start = pl.multiple_of(flip(place, j, 2) * width, width)
        loads.append(
            pltpu.make_async_copy(w_hbm.at[0, pl.ds(start, width)], w_v.at[j], local_sem.at[j])
        )
    cot_loads = []
    for p in range(8):
        start = pl.multiple_of(peers[p] * cap, cap)
        cot_loads.append(
            pltpu.make_async_copy(
                cot_hbm.at[0, pl.ds(start, cap)], cot_v.at[p], local_sem.at[4 + p]
            )
        )

    position = lax.broadcasted_iota(jnp.int32, (1, tok), 1)
    limit = jnp.zeros((1, tok), jnp.int32)
    inputs[0].wait()
    for i in range(lengths_ref.shape[0]):
        limit = jnp.where(position // SEQ_LEN == i, lengths_ref[i], limit)
    live = position % SEQ_LEN < limit
    away = jnp.bitwise_xor(ids_ref[...], expert)
    rank_of = jnp.zeros((1, tok), jnp.int32)
    for p, k in enumerate(ORDER):
        rank_of = jnp.where(away == k, p, rank_of)
    rank_of = jnp.where(live, rank_of, -1)
    onehot = jnp.where(
        lax.broadcasted_iota(jnp.int32, (16, tok), 0) == rank_of, 1.0, 0.0
    )
    before = lax.broadcasted_iota(jnp.int32, (tok, tok), 0) <= lax.broadcasted_iota(
        jnp.int32, (tok, tok), 1
    )
    counts = jnp.dot(
        onehot.astype(jnp.bfloat16),
        jnp.where(before, 1.0, 0.0).astype(jnp.bfloat16),
        preferred_element_type=jnp.float32,
    )
    slot = jnp.sum(counts * onehot, axis=0, keepdims=True) - 1.0
    slot = jnp.where(live, slot + (rank_of * cap).astype(jnp.float32), -1.0)
    slots = lax.broadcasted_iota(jnp.int32, (8 * cap, tok), 0).astype(jnp.float32)
    chosen = jnp.where(slots == slot, 1.0, 0.0)
    inputs[1].wait()
    placed = jnp.dot(
        chosen.astype(jnp.bfloat16), tokens_ref[...], preferred_element_type=jnp.float32
    ).astype(jnp.bfloat16)
    feats[0, 0] = placed[:cap]
    for p in range(1, 8):
        send_rows[p] = placed[p * cap : (p + 1) * cap]

    pl.semaphore_wait(barrier, len(greeted))

    started = []
    numbers = iter(range(1000))

    def remote(source, target, device):
        n = next(numbers)
        return pltpu.make_async_remote_copy(
            src_ref=source,
            dst_ref=target,
            send_sem=send_sem.at[n],
            recv_sem=recv_sem.at[n],
            device_id=device,
            device_id_type=MESH,
        )

    def go(copy):
        copy.start()
        started.append(copy)

    out_copies = [None] + [
        remote(send_rows.at[p], feats.at[0, p], (peers[p], place)) for p in range(1, 8)
    ]
    back_copies = [None] + [
        remote(done_rows.at[p], back_rows.at[p], (peers[p], place)) for p in range(1, 8)
    ]
    pairs = [pl.ds(2 * q, 2) for q in range(4)]
    gather = [
        [None] + [remote(feats.at[0, pair], feats.at[d, pair], side[d]) for d in (1, 2)]
        for pair in pairs[1:]
    ]
    gather = [None] + gather
    relay = [
        [
            None,
            remote(feats.at[2, pair, second], feats.at[3, pair, second], side[1]),
            remote(feats.at[1, pair, first], feats.at[3, pair, first], side[2]),
        ]
        for pair in pairs
    ]
    rows = [None, first, second]
    diag = [
        [None]
        + [remote(parts.at[3, pair, rows[d]], diag_in.at[d - 1, pair], side[d]) for d in (1, 2)]
        for pair in pairs
    ]
    direct = [
        [None]
        + [remote(parts.at[d, pair, rows[d]], direct_in.at[d - 1, pair], side[d]) for d in (1, 2)]
        for pair in pairs
    ]
    summed = [
        [None]
        + [remote(sum_out.at[d - 1, pair], sum_in.at[d - 1, pair], side[d]) for d in (1, 2)]
        for pair in pairs
    ]

    own = [None] + [remote(feats.at[0, 0], feats.at[d, 0], side[d]) for d in (1, 2)]
    peer = [None] + [remote(feats.at[0, 1], feats.at[d, 1], side[d]) for d in (1, 2)]
    go(own[1])
    go(own[2])
    for p in (1, 2, 3):
        go(out_copies[p])
    for load in cot_loads:
        load.start()

    def gather_start(q):
        if q == 0:
            out_copies[1].wait_recv()
            go(peer[1])
            go(peer[2])
            return
        out_copies[2 * q].wait_recv()
        out_copies[2 * q + 1].wait_recv()
        go(gather[q][1])
        go(gather[q][2])

    def gather_relay(q):
        for d in (1, 2):
            if q == 0:
                own[d].wait_recv()
                peer[d].wait_recv()
            else:
                gather[q][d].wait_recv()
            go(relay[q][3 - d])

    def gather_end(q):
        relay[q][1].wait_recv()
        relay[q][2].wait_recv()

    rows_all = 4 * cap

    def hidden_tile(g, n):
        group, columns = slice(4 * g, 4 * g + 4), slice(n * TILE, (n + 1) * TILE)
        total = None
        for j in range(4):
            product = jnp.dot(
                feats[j, group].reshape(rows_all, width),
                w_v[j, :, columns],
                preferred_element_type=jnp.float32,
            )
            total = product if total is None else total + product
        cotangent = cot_v[group, :, columns].reshape(rows_all, TILE).astype(jnp.float32)
        hidden[:, columns] = (cotangent * gelu_slope(total)).astype(jnp.bfloat16)

    def part_block(g, j):
        group = slice(4 * g, 4 * g + 4)
        for n in range(width // TILE):
            columns = slice(n * TILE, (n + 1) * TILE)
            block = lax.dot_general(
                w_v[j, columns, :],
                hidden[...],
                (((1,), (1,)), ((), ())),
                preferred_element_type=jnp.float32,
            )
            parts[j, group, :, columns] = block.T.astype(jnp.bfloat16).reshape(4, cap, TILE)

    def sum_step(q, d):
        pair, other = pairs[q], 3 - d
        diag[q][d].wait_recv()
        sum_out[other - 1, pair] = (
            parts[other, pair, rows[d]].astype(jnp.float32)
            + diag_in[d - 1, pair].astype(jnp.float32)
        ).astype(jnp.bfloat16)
        go(summed[q][other])

    def final_step(q):
        pair = pairs[q]
        for d in (1, 2):
            direct[q][d].wait_recv()
            summed[q][3 - d].wait_recv()
            total = (
                parts[0, pair, rows[d]].astype(jnp.float32)
                + direct_in[d - 1, pair].astype(jnp.float32)
                + sum_in[2 - d, pair].astype(jnp.float32)
            ).astype(jnp.bfloat16)
            done_rows[pair, rows[d]] = total
        for p in (2 * q, 2 * q + 1):
            if p:
                go(back_copies[p])
            else:
                back_rows[0] = done_rows[0]

    tiles = ff // TILE
    gather_start(0)
    loads[0].start()
    combine[...] = chosen.T.astype(jnp.bfloat16)
    gather_relay(0)
    loads[1].start()
    gather_start(1)
    for p in (6, 7, 4, 5):
        go(out_copies[p])
    loads[2].start()
    gather_relay(1)
    loads[3].start()
    gather_start(2)
    for load in loads + cot_loads:
        load.wait()
    gather_end(0)
    gather_end(1)
    hidden_tile(0, 0)
    gather_relay(2)
    gather_start(3)
    for n in range(1, tiles):
        hidden_tile(0, n)
    gather_relay(3)
    part_block(0, 3)
    for q in RETURN[2:]:
        go(diag[q][1])
        go(diag[q][2])
    for j in (1, 2, 0):
        part_block(0, j)
    for q in RETURN[2:]:
        sum_step(q, 2)
        sum_step(q, 1)
        go(direct[q][1])
        go(direct[q][2])
    gather_end(2)
    gather_end(3)
    for n in range(tiles):
        hidden_tile(1, n)
    part_block(1, 3)
    for q in RETURN[:2]:
        go(diag[q][1])
        go(diag[q][2])
    final_step(RETURN[2])
    for j in (1, 2):
        part_block(1, j)
    for q in RETURN[:2]:
        sum_step(q, 2)
        sum_step(q, 1)
        go(direct[q][1])
        go(direct[q][2])
    final_step(RETURN[3])
    part_block(1, 0)
    for q in RETURN[:2]:
        final_step(q)
    for p in range(1, 8):
        back_copies[p].wait_recv()
    out_ref[...] = jnp.dot(
        combine[...],
        back_rows[...].reshape(8 * cap, width),
        preferred_element_type=jnp.float32,
    ).astype(out_ref.dtype)
    for copy in started:
        copy.wait_send()


def one_kernel(tokens, expert_ids, seq_lengths, hidden_cotangent, w_in):
    tok, width = tokens.shape
    ff = w_in.shape[2]
    cap = hidden_cotangent.shape[1] // 8
    half = cap // 2
    bf16 = jnp.bfloat16
    copies = 7 + 7 + 4 * 10 + 2
    vmem, anywhere = pl.BlockSpec(memory_space=pltpu.VMEM), pl.BlockSpec(memory_space=pl.ANY)
    smem = pl.BlockSpec(memory_space=pltpu.SMEM)
    return pl.pallas_call(
        functools.partial(kernel, cap),
        out_shape=jax.ShapeDtypeStruct((tok, width), tokens.dtype),
        in_specs=[anywhere, anywhere, smem, anywhere, anywhere],
        out_specs=vmem,
        scratch_shapes=[
            pltpu.VMEM((tok, width), bf16),
            pltpu.VMEM((1, tok), jnp.int32),
            pltpu.VMEM((4, width, ff), bf16),
            pltpu.VMEM((8, cap, ff), bf16),
            pltpu.VMEM((8, cap, width), bf16),
            pltpu.VMEM((4, 8, cap, width), bf16),
            pltpu.VMEM((4, 8, cap, width), bf16),
            pltpu.VMEM((4 * cap, ff), bf16),
            pltpu.VMEM((tok, 8 * cap), bf16),
            pltpu.VMEM((2, 8, half, width), bf16),
            pltpu.VMEM((2, 8, half, width), bf16),
            pltpu.VMEM((2, 8, half, width), bf16),
            pltpu.VMEM((2, 8, half, width), bf16),
            pltpu.VMEM((8, cap, width), bf16),
            pltpu.VMEM((8, cap, width), bf16),
            pltpu.SemaphoreType.DMA((14,)),
            pltpu.SemaphoreType.DMA((copies,)),
            pltpu.SemaphoreType.DMA((copies,)),
        ],
        compiler_params=pltpu.CompilerParams(
            collective_id=0, has_side_effects=True, vmem_limit_bytes=58 << 20
        ),
        cost_estimate=pl.CostEstimate(
            flops=4 * 8 * cap * 4 * width * ff,
            bytes_accessed=2 * 4 * width * ff,
            transcendentals=8 * cap * ff,
        ),
    )(tokens, expert_ids.reshape(1, tok), seq_lengths, hidden_cotangent, w_in)


def solution(mesh):
    in_specs = (
        P("expert", "mp"),
        P("expert", None),
        P("expert"),
        P("expert", None, "mp"),
        P("expert", None, "mp"),
    )
    out_specs = P("expert", "mp")
    small = mesh.shape["mp"] == 4 and mesh.shape["expert"] == 8
    return jax.shard_map(
        one_kernel if small else per_device,
        mesh=mesh,
        in_specs=in_specs,
        out_specs=out_specs,
        check_vma=False,
    )
```

```python
import functools
import math

import jax
import jax.numpy as jnp
from jax import lax
from jax.experimental import pallas as pl
from jax.experimental.pallas import tpu as pltpu
from jax.sharding import PartitionSpec as P

SEQ_LEN = 128
MESH = pl.DeviceIdType.MESH
ORDER = (0, 1, 4, 5, 2, 3, 6, 7)
RETURN = (3, 2, 1, 0)
TILE = 512
def gelu_slope(preact):
    coeff = math.sqrt(2.0 / math.pi)
    squashed = jnp.tanh(coeff * (preact + 0.044715 * preact * preact * preact))
    return 0.5 * (1.0 + squashed) + 0.5 * preact * (1.0 - squashed * squashed) * coeff * (
        1.0 + 3.0 * 0.044715 * preact * preact
    )


def per_device(tokens, expert_ids, seq_lengths, hidden_cotangent, w_in):
    tok_dev = tokens.shape[0]
    experts = w_in.shape[0] * lax.axis_size("expert")
    capacity = max(2, 2 * tok_dev // experts)
    position = jnp.arange(tok_dev, dtype=jnp.int32)
    seq_index = position // SEQ_LEN
    seq_length = jnp.sum(
        jnp.where(
            seq_index[:, None] == jnp.arange(seq_lengths.shape[0], dtype=jnp.int32)[None, :],
            seq_lengths[None, :],
            0,
        ),
        axis=1,
    )
    live_mask = position % SEQ_LEN < seq_length
    expert_row = expert_ids[:, 0]
    onehot = (
        (expert_row[:, None] == jnp.arange(experts, dtype=jnp.int32)[None, :]) & live_mask[:, None]
    ).astype(jnp.int32)
    slot_rank = jnp.sum(jnp.cumsum(onehot, axis=0) * onehot, axis=1) - 1
    target = jnp.where(live_mask, expert_row * capacity + slot_rank, experts * capacity)
    buffer = (
        jnp.zeros((experts * capacity + 1,) + tokens.shape[1:], tokens.dtype).at[target].set(tokens)
    )
    arrived = lax.all_to_all(
        buffer[:-1].reshape((experts, capacity) + tokens.shape[1:]),
        "expert",
        split_axis=0,
        concat_axis=0,
        tiled=True,
    )
    slot_count = arrived.shape[0] * capacity
    features = lax.all_gather(
        arrived.reshape(slot_count, arrived.shape[2]), "mp", axis=1, tiled=True
    )
    weight = w_in[0]
    pre_act = jnp.dot(features, weight, preferred_element_type=jnp.float32)
    hidden_grad = (hidden_cotangent[0].astype(jnp.float32) * gelu_slope(pre_act)).astype(
        jnp.bfloat16
    )
    partial_value = lax.dot_general(
        hidden_grad, weight, (((1,), (1,)), ((), ())), preferred_element_type=jnp.float32
    ).astype(jnp.bfloat16)
    partial_value = lax.optimization_barrier(partial_value)
    summed = lax.psum_scatter(
        partial_value.astype(jnp.float32).astype(jnp.bfloat16),
        "mp",
        scatter_dimension=1,
        tiled=True,
    )
    returned = lax.all_to_all(
        summed.reshape(arrived.shape[0], capacity, summed.shape[1]),
        "expert",
        split_axis=0,
        concat_axis=0,
        tiled=True,
    )
    flat_rows = returned.reshape((experts * capacity,) + returned.shape[2:])
    padded = jnp.concatenate(
        [flat_rows, jnp.zeros((1,) + flat_rows.shape[1:], flat_rows.dtype)], axis=0
    )
    return padded[target]


def flip(index, difference, bits):
    total = 0
    for bit in range(bits):
        value = lax.rem(index // (1 << bit), 2)
        total = total + (1 << bit) * ((1 - value) if difference >> bit & 1 else value)
    return total


def kernel(
    cap,
    tokens_hbm,
    ids_hbm,
    lengths_ref,
    cot_hbm,
    w_hbm,
    out_ref,
    tokens_ref,
    ids_ref,
    w_v,
    cot_v,
    send_rows,
    feats,
    parts,
    hidden,
    combine,
    diag_in,
    direct_in,
    sum_in,
    sum_out,
    done_rows,
    back_rows,
    local_sem,
    send_sem,
    recv_sem,
):
    expert, place = lax.axis_index("expert"), lax.axis_index("mp")
    peers = [flip(expert, k, 3) for k in ORDER]
    side = [None, (expert, flip(place, 1, 2)), (expert, flip(place, 2, 2))]
    tok, width = tokens_ref.shape
    ff = w_v.shape[2]
    half = cap // 2
    first, second = pl.ds(0, half), pl.ds(half, half)

    barrier = pltpu.get_barrier_semaphore()
    greeted = [(peer, place) for peer in peers[1:]] + side[1:]
    for device in greeted:
        pl.semaphore_signal(barrier, inc=1, device_id=device, device_id_type=MESH)

    inputs = [
        pltpu.make_async_copy(source, target, local_sem.at[12 + n])
        for n, (source, target) in enumerate(
            ((ids_hbm, ids_ref), (tokens_hbm, tokens_ref))
        )
    ]
    for load in inputs:
        load.start()
    loads = []
    for j in range(4):
        start = pl.multiple_of(flip(place, j, 2) * width, width)
        loads.append(
            pltpu.make_async_copy(w_hbm.at[0, pl.ds(start, width)], w_v.at[j], local_sem.at[j])
        )
    cot_loads = []
    for p in range(8):
        start = pl.multiple_of(peers[p] * cap, cap)
        cot_loads.append(
            pltpu.make_async_copy(
                cot_hbm.at[0, pl.ds(start, cap)], cot_v.at[p], local_sem.at[4 + p]
            )
        )

    position = lax.broadcasted_iota(jnp.int32, (1, tok), 1)
    limit = jnp.zeros((1, tok), jnp.int32)
    inputs[0].wait()
    for i in range(lengths_ref.shape[0]):
        limit = jnp.where(position // SEQ_LEN == i, lengths_ref[i], limit)
    live = position % SEQ_LEN < limit
    away = jnp.bitwise_xor(ids_ref[...], expert)
    rank_of = jnp.zeros((1, tok), jnp.int32)
    for p, k in enumerate(ORDER):
        rank_of = jnp.where(away == k, p, rank_of)
    rank_of = jnp.where(live, rank_of, -1)
    onehot = jnp.where(
        lax.broadcasted_iota(jnp.int32, (16, tok), 0) == rank_of, 1.0, 0.0
    )
    before = lax.broadcasted_iota(jnp.int32, (tok, tok), 0) <= lax.broadcasted_iota(
        jnp.int32, (tok, tok), 1
    )
    counts = jnp.dot(
        onehot.astype(jnp.bfloat16),
        jnp.where(before, 1.0, 0.0).astype(jnp.bfloat16),
        preferred_element_type=jnp.float32,
    )
    slot = jnp.sum(counts * onehot, axis=0, keepdims=True) - 1.0
    slot = jnp.where(live, slot + (rank_of * cap).astype(jnp.float32), -1.0)
    slots = lax.broadcasted_iota(jnp.int32, (8 * cap, tok), 0).astype(jnp.float32)
    chosen = jnp.where(slots == slot, 1.0, 0.0)
    inputs[1].wait()
    placed = jnp.dot(
        chosen.astype(jnp.bfloat16), tokens_ref[...], preferred_element_type=jnp.float32
    ).astype(jnp.bfloat16)
    feats[0, 0] = placed[:cap]
    for p in range(1, 8):
        send_rows[p] = placed[p * cap : (p + 1) * cap]

    pl.semaphore_wait(barrier, len(greeted))

    started = []
    numbers = iter(range(1000))

    def remote(source, target, device):
        n = next(numbers)
        return pltpu.make_async_remote_copy(
            src_ref=source,
            dst_ref=target,
            send_sem=send_sem.at[n],
            recv_sem=recv_sem.at[n],
            device_id=device,
            device_id_type=MESH,
        )

    def go(copy):
        copy.start()
        started.append(copy)

    out_copies = [None] + [
        remote(send_rows.at[p], feats.at[0, p], (peers[p], place)) for p in range(1, 8)
    ]
    back_copies = [None] + [
        remote(done_rows.at[p], back_rows.at[p], (peers[p], place)) for p in range(1, 8)
    ]
    pairs = [pl.ds(2 * q, 2) for q in range(4)]
    gather = [
        [None] + [remote(feats.at[0, pair], feats.at[d, pair], side[d]) for d in (1, 2)]
        for pair in pairs[1:]
    ]
    gather = [None] + gather
    relay = [
        [
            None,
            remote(feats.at[2, pair, second], feats.at[3, pair, second], side[1]),
            remote(feats.at[1, pair, first], feats.at[3, pair, first], side[2]),
        ]
        for pair in pairs
    ]
    rows = [None, first, second]
    diag = [
        [None]
        + [remote(parts.at[3, pair, rows[d]], diag_in.at[d - 1, pair], side[d]) for d in (1, 2)]
        for pair in pairs
    ]
    direct = [
        [None]
        + [remote(parts.at[d, pair, rows[d]], direct_in.at[d - 1, pair], side[d]) for d in (1, 2)]
        for pair in pairs
    ]
    summed = [
        [None]
        + [remote(sum_out.at[d - 1, pair], sum_in.at[d - 1, pair], side[d]) for d in (1, 2)]
        for pair in pairs
    ]

    own = [None] + [remote(feats.at[0, 0], feats.at[d, 0], side[d]) for d in (1, 2)]
    peer = [None] + [remote(feats.at[0, 1], feats.at[d, 1], side[d]) for d in (1, 2)]
    go(own[1])
    go(own[2])
    for p in (1, 2, 3):
        go(out_copies[p])
    for load in cot_loads:
        load.start()

    def gather_start(q):
        if q == 0:
            out_copies[1].wait_recv()
            go(peer[1])
            go(peer[2])
            return
        out_copies[2 * q].wait_recv()
        out_copies[2 * q + 1].wait_recv()
        go(gather[q][1])
        go(gather[q][2])

    def gather_relay(q):
        for d in (1, 2):
            if q == 0:
                own[d].wait_recv()
                peer[d].wait_recv()
            else:
                gather[q][d].wait_recv()
            go(relay[q][3 - d])

    def gather_end(q):
        relay[q][1].wait_recv()
        relay[q][2].wait_recv()

    rows_all = 4 * cap

    def hidden_tile(g, n):
        group, columns = slice(4 * g, 4 * g + 4), slice(n * TILE, (n + 1) * TILE)
        total = None
        for j in range(4):
            product = jnp.dot(
                feats[j, group].reshape(rows_all, width),
                w_v[j, :, columns],
                preferred_element_type=jnp.float32,
            )
            total = product if total is None else total + product
        cotangent = cot_v[group, :, columns].reshape(rows_all, TILE).astype(jnp.float32)
        hidden[:, columns] = (cotangent * gelu_slope(total)).astype(jnp.bfloat16)

    def part_block(g, j):
        group = slice(4 * g, 4 * g + 4)
        for n in range(width // TILE):
            columns = slice(n * TILE, (n + 1) * TILE)
            block = lax.dot_general(
                w_v[j, columns, :],
                hidden[...],
                (((1,), (1,)), ((), ())),
                preferred_element_type=jnp.float32,
            )
            parts[j, group, :, columns] = block.T.astype(jnp.bfloat16).reshape(4, cap, TILE)

    def sum_step(q, d):
        pair, other = pairs[q], 3 - d
        diag[q][d].wait_recv()
        sum_out[other - 1, pair] = (
            parts[other, pair, rows[d]].astype(jnp.float32)
            + diag_in[d - 1, pair].astype(jnp.float32)
        ).astype(jnp.bfloat16)
        go(summed[q][other])

    def final_step(q):
        pair = pairs[q]
        for d in (1, 2):
            direct[q][d].wait_recv()
            summed[q][3 - d].wait_recv()
            total = (
                parts[0, pair, rows[d]].astype(jnp.float32)
                + direct_in[d - 1, pair].astype(jnp.float32)
                + sum_in[2 - d, pair].astype(jnp.float32)
            ).astype(jnp.bfloat16)
            done_rows[pair, rows[d]] = total
        for p in (2 * q, 2 * q + 1):
            if p:
                go(back_copies[p])
            else:
                back_rows[0] = done_rows[0]

    tiles = ff // TILE
    gather_start(0)
    loads[0].start()
    combine[...] = chosen.T.astype(jnp.bfloat16)
    gather_relay(0)
    loads[1].start()
    gather_start(1)
    for p in (6, 7, 4, 5):
        go(out_copies[p])
    loads[2].start()
    gather_relay(1)
    loads[3].start()
    gather_start(2)
    for load in loads + cot_loads:
        load.wait()
    gather_end(0)
    gather_end(1)
    hidden_tile(0, 0)
    gather_relay(2)
    gather_start(3)
    for n in range(1, tiles - 1):
        hidden_tile(0, n)
    gather_relay(3)
    hidden_tile(0, tiles - 1)
    part_block(0, 3)
    for q in RETURN[2:]:
        go(diag[q][1])
        go(diag[q][2])
    for j in (1, 2):
        part_block(0, j)
        for q in RETURN[2:]:
            go(direct[q][j])
    part_block(0, 0)
    gather_end(2)
    gather_end(3)
    hidden_tile(1, 0)
    for q in RETURN[2:]:
        sum_step(q, 2)
        sum_step(q, 1)
    for n in range(1, tiles):
        hidden_tile(1, n)
    part_block(1, 3)
    for q in RETURN[:2]:
        go(diag[q][1])
        go(diag[q][2])
    final_step(RETURN[2])
    for j in (1, 2):
        part_block(1, j)
    for q in RETURN[:2]:
        sum_step(q, 2)
        sum_step(q, 1)
        go(direct[q][1])
        go(direct[q][2])
    final_step(RETURN[3])
    part_block(1, 0)
    for q in RETURN[:2]:
        final_step(q)
    for p in range(1, 8):
        back_copies[p].wait_recv()
    out_ref[...] = jnp.dot(
        combine[...],
        back_rows[...].reshape(8 * cap, width),
        preferred_element_type=jnp.float32,
    ).astype(out_ref.dtype)
    for copy in started:
        copy.wait_send()


def one_kernel(tokens, expert_ids, seq_lengths, hidden_cotangent, w_in):
    tok, width = tokens.shape
    ff = w_in.shape[2]
    cap = hidden_cotangent.shape[1] // 8
    half = cap // 2
    bf16 = jnp.bfloat16
    copies = 7 + 7 + 4 * 10 + 2
    vmem, anywhere = pl.BlockSpec(memory_space=pltpu.VMEM), pl.BlockSpec(memory_space=pl.ANY)
    smem = pl.BlockSpec(memory_space=pltpu.SMEM)
    return pl.pallas_call(
        functools.partial(kernel, cap),
        out_shape=jax.ShapeDtypeStruct((tok, width), tokens.dtype),
        in_specs=[anywhere, anywhere, smem, anywhere, anywhere],
        out_specs=vmem,
        scratch_shapes=[
            pltpu.VMEM((tok, width), bf16),
            pltpu.VMEM((1, tok), jnp.int32),
            pltpu.VMEM((4, width, ff), bf16),
            pltpu.VMEM((8, cap, ff), bf16),
            pltpu.VMEM((8, cap, width), bf16),
            pltpu.VMEM((4, 8, cap, width), bf16),
            pltpu.VMEM((4, 8, cap, width), bf16),
            pltpu.VMEM((4 * cap, ff), bf16),
            pltpu.VMEM((tok, 8 * cap), bf16),
            pltpu.VMEM((2, 8, half, width), bf16),
            pltpu.VMEM((2, 8, half, width), bf16),
            pltpu.VMEM((2, 8, half, width), bf16),
            pltpu.VMEM((2, 8, half, width), bf16),
            pltpu.VMEM((8, cap, width), bf16),
            pltpu.VMEM((8, cap, width), bf16),
            pltpu.SemaphoreType.DMA((14,)),
            pltpu.SemaphoreType.DMA((copies,)),
            pltpu.SemaphoreType.DMA((copies,)),
        ],
        compiler_params=pltpu.CompilerParams(
            collective_id=0, has_side_effects=True, vmem_limit_bytes=58 << 20
        ),
        cost_estimate=pl.CostEstimate(
            flops=4 * 8 * cap * 4 * width * ff,
            bytes_accessed=2 * 4 * width * ff,
            transcendentals=8 * cap * ff,
        ),
    )(tokens, expert_ids.reshape(1, tok), seq_lengths, hidden_cotangent, w_in)


def solution(mesh):
    in_specs = (
        P("expert", "mp"),
        P("expert", None),
        P("expert"),
        P("expert", None, "mp"),
        P("expert", None, "mp"),
    )
    out_specs = P("expert", "mp")
    small = mesh.shape["mp"] == 4 and mesh.shape["expert"] == 8
    return jax.shard_map(
        one_kernel if small else per_device,
        mesh=mesh,
        in_specs=in_specs,
        out_specs=out_specs,
        check_vma=False,
    )
```
